32 devices in a mesh: seq: 4 (over x, core), dp: 8 (over z, y).
Axes of the slice: x: 2, y: 2, z: 4, core: 2. Of those that a mesh axis runs over, the one named last changes fastest.
Arguments:
- tokens: bfloat16 [8, 1024, 1536], P('dp', 'seq'), may hold values from -6 to 6
- seg_flags: int32 [8, 1024], P('dp'), may hold values from 0 to 1, as said below
- routes: int32 [8, 1024, 6], P('dp', 'seq'), may hold values from 0 to 15, all different within a row; in each aligned block of 256 rows (0 to 255, 256 to 511, ..., all dimensions but the last counted through in order) at most 128 rows name the same one
- out_grad: bfloat16 [8, 1024, 1536], P('dp', 'seq'), may hold values from -6 to 6
- w_in: float32 [1536, 6448], P(('seq', 'dp')), may hold values from -0.15625 to 0.15625
- w_in_m: float32 [1536, 6448], P(('seq', 'dp')), may hold values from -24 to 24
- w_in_v: float32 [1536, 6448], P(('seq', 'dp')), may hold values from 68.8128 to 278.528
- w_router: float32 [1536, 16], P(('seq', 'dp')), may hold values from -0.078125 to 0.078125
- w_router_m: float32 [1536, 16], P(('seq', 'dp')), may hold values from -384 to 384
- w_router_v: float32 [1536, 16], P(('seq', 'dp')), may hold values from 16281.6 to 64512
- w_shared_in: float32 [1536, 2048], P(('seq', 'dp')), may hold values from -0.15625 to 0.15625
- w_shared_in_m: float32 [1536, 2048], P(('seq', 'dp')), may hold values from -32 to 32
- w_shared_in_v: float32 [1536, 2048], P(('seq', 'dp')), may hold values from 155.648 to 622.592
- w_out: float32 [3072, 1536], P(('seq', 'dp')), may hold values from -0.109375 to 0.109375
- w_out_m: float32 [3072, 1536], P(('seq', 'dp')), may hold values from -64 to 64
- w_out_v: float32 [3072, 1536], P(('seq', 'dp')), may hold values from 622.592 to 2457.6
- w_shared_out: float32 [1024, 1536], P(('seq', 'dp')), may hold values from -0.1875 to 0.1875
- w_shared_out_m: float32 [1024, 1536], P(('seq', 'dp')), may hold values from -32 to 32
- w_shared_out_v: float32 [1024, 1536], P(('seq', 'dp')), may hold values from 155.648 to 622.592
- w_experts_in: float32 [16, 1536, 1024], P('dp', 'seq'), may hold values from -0.15625 to 0.15625
- w_experts_in_m: float32 [16, 1536, 1024], P('dp', 'seq'), may hold values from -16 to 16
- w_experts_in_v: float32 [16, 1536, 1024], P('dp', 'seq'), may hold values from 28.5696 to 113.664
- w_experts_out: float32 [16, 512, 1536], P('dp', 'seq'), may hold values from -0.625 to 0.625
- w_experts_out_m: float32 [16, 512, 1536], P('dp', 'seq'), may hold values from -4 to 4
- w_experts_out_v: float32 [16, 512, 1536], P('dp', 'seq'), may hold values from 1.62816 to 6.4512
- small_params: float32 [22928], replicated, may hold values from -6.9 to 1.5, as said below
- small_m: float32 [22928], replicated, may hold values from -32 to 32
- small_v: float32 [22928], replicated, may hold values from 106.496 to 434.176
Outputs:
- block_out: bfloat16 [8, 1024, 1536], P('dp', 'seq')
- input_grad: float32 [8, 1024, 1536], P('dp', 'seq')
- new_w_in: float32 [1536, 6448], P(('seq', 'dp'))
- new_w_in_m: float32 [1536, 6448], P(('seq', 'dp'))
- new_w_in_v: float32 [1536, 6448], P(('seq', 'dp'))
- new_w_router: float32 [1536, 16], P(('seq', 'dp'))
- new_w_router_m: float32 [1536, 16], P(('seq', 'dp'))
- new_w_router_v: float32 [1536, 16], P(('seq', 'dp'))
- new_w_shared_in: float32 [1536, 2048], P(('seq', 'dp'))
- new_w_shared_in_m: float32 [1536, 2048], P(('seq', 'dp'))
- new_w_shared_in_v: float32 [1536, 2048], P(('seq', 'dp'))
- new_w_out: float32 [3072, 1536], P(('seq', 'dp'))
- new_w_out_m: float32 [3072, 1536], P(('seq', 'dp'))
- new_w_out_v: float32 [3072, 1536], P(('seq', 'dp'))
- new_w_shared_out: float32 [1024, 1536], P(('seq', 'dp'))
- new_w_shared_out_m: float32 [1024, 1536], P(('seq', 'dp'))
- new_w_shared_out_v: float32 [1024, 1536], P(('seq', 'dp'))
- new_w_experts_in: float32 [16, 1536, 1024], P('dp', 'seq')
- new_w_experts_in_m: float32 [16, 1536, 1024], P('dp', 'seq')
- new_w_experts_in_v: float32 [16, 1536, 1024], P('dp', 'seq')
- new_w_experts_out: float32 [16, 512, 1536], P('dp', 'seq')
- new_w_experts_out_m: float32 [16, 512, 1536], P('dp', 'seq')
- new_w_experts_out_v: float32 [16, 512, 1536], P('dp', 'seq')
- new_small: float32 [22928], replicated
- new_small_m: float32 [22928], replicated
- new_small_v: float32 [22928], replicated
The draws below stay inside these ranges and needn't reach their ends.
Inputs may be any that keep to these rules, and one draw needn't show every extreme that they name: `seg_flags`: positions count from 0. Each row starts a document at position 0; in each row one document starts at a position p from 1 to 128, the next start q lies between 896 and 1023, and no document starts between p and q. `routes`: in the rows of one device no expert is named by more than 128 rows; a row names different experts. `small_params`: norm gains lie between 0.55 and 1.45, dt_bias between -5 and -3, a_log between -6.9 and 0.7, d_skip between 0.5 and 1.5.
All inputs are finite; a program needn't handle non-finite values.
Results may differ from the reference program's by a relative error of at most 0.017.
Values may be sent and summed in bfloat16 or wider, within the bound.
A program may use at most 224 MiB of HBM per device.

```python
import math
import jax
import jax.numpy as jnp
import numpy as np
from jax import lax

D = 1536
HEADS = 48
HEAD_DIM = 64
STATE = 128
KCONV = 4
EF = 512
SF = 1024
TOPK = 6
STEP = 10
TOK_DEV = 256
DI = 3072
XBC = 3328
PROJ = 6448
SMALL = 22928
EXPERTS = 16
CAP = 128
ROWS = 8
ROW_LEN = 1024
TOKENS_ALL = 8192


def draw_seg_flags(key, part):
    key = jax.random.fold_in(key, 11)
    subkeys = jax.random.split(key, 3)
    doc_begin = jax.random.randint(subkeys[0], (ROWS, 1), 1, TOK_DEV // 2 + 1)
    doc_after = jax.random.randint(subkeys[1], (ROWS, 1), ROW_LEN - TOK_DEV // 2, ROW_LEN)
    places = jnp.arange(ROW_LEN)[None, :]
    sparse = jax.random.randint(subkeys[2], (ROWS, ROW_LEN), 0, 24) == 0
    outside = (places < doc_begin) | (places > doc_after)
    starts = (places == 0) | (places == doc_begin) | (places == doc_after) | sparse & outside
    return starts.astype(jnp.int32)


def draw_small_params(key, part):
    key = jax.random.fold_in(key, 5)
    subkeys = jax.random.split(key, 6)
    count = 2 * D + DI
    gains = 1.0 + 0.15 * jnp.clip(jax.random.normal(subkeys[0], (count,), jnp.float32), -3.0, 3.0)
    conv_weight = 0.5 * jnp.clip(jax.random.normal(subkeys[1], (KCONV * XBC,), jnp.float32), -3.0, 3.0)
    conv_bias = 0.3 * jnp.clip(jax.random.normal(subkeys[2], (XBC,), jnp.float32), -3.0, 3.0)
    dt_bias = jax.random.uniform(subkeys[3], (HEADS,), jnp.float32, -5.0, -3.0)
    a_log = jax.random.uniform(subkeys[4], (HEADS,), jnp.float32, -6.9, 0.7)
    d_skip = jax.random.uniform(subkeys[5], (HEADS,), jnp.float32, 0.5, 1.5)
    return jnp.concatenate([gains[:D], conv_weight, conv_bias, dt_bias, a_log, d_skip, gains[D:D + DI], gains[D + DI:]], 0)


def block_levels(stream_key, dims, cuts, smallest, high):
    def one(dim, blocks):
        steps = jax.random.uniform(jax.random.fold_in(jax.random.fold_in(stream_key, 6), dim), (blocks,), jnp.float32, smallest / len(cuts), high / len(cuts))
        return jnp.repeat(jnp.exp(steps), dims[dim] // blocks).reshape((-1,) + (1,) * (len(dims) - dim - 1))

    level = one(*cuts[0])
    for cut in cuts[1:]:
        level = level * one(*cut)
    return level


def assign_block(stream_key, own, number, rows, number_of, top, bound, lean):
    sequence = jax.random.permutation(stream_key, number_of)
    heavy_load, ordinary = portions_of(number_of, rows * top, bound, lean, True), portions_of(number_of, rows * top, bound, lean, False)
    places = jnp.arange(number_of)

    def named(sizes, turn):
        used = int((sizes > 0).sum())
        fixed = max(1, used // 4)
        shifted = fixed + (places - fixed + turn * (used - fixed)) % max(1, number_of - fixed)
        return jnp.zeros((number_of,), jnp.int32).at[sequence[jnp.where(places < fixed, places, shifted)]].set(jnp.asarray(sizes, jnp.int32))

    sizes = jnp.where(number % 4 == 0, named(heavy_load, number // 4), named(ordinary, number - number // 4 - 1))
    mixed = jax.random.permutation(jax.random.fold_in(own, 3), number_of)
    giver, receiver = mixed[0:number_of // 2 * 2:2], mixed[1:number_of // 2 * 2:2]
    room = jnp.minimum(sizes[giver] - 1, bound - sizes[receiver]) // 2
    room = jnp.where((giver == sequence[0]) | (receiver == sequence[0]) | (sizes[receiver] == 0), 0, jnp.maximum(room, 0))
    shifted = jax.random.randint(jax.random.fold_in(own, 4), (number_of // 2,), 0, 1 << 20) % (room + 1)
    sizes = sizes.at[giver].add(-shifted).at[receiver].add(shifted)
    members = jnp.searchsorted(jnp.cumsum(sizes), jnp.arange(rows * top), side="right").astype(jnp.int32)
    grid = members.reshape(top, rows).T
    grid = grid[jax.random.permutation(jax.random.fold_in(own, 1), rows)]
    turn = jax.random.randint(jax.random.fold_in(own, 2), (rows, 1), 0, top)
    return jnp.take_along_axis(grid, (jnp.arange(top)[None, :] + turn) % top, axis=1)


def portions_of(amount, total, limit, slope, full):
    portions = [(1 << 20) // math.isqrt(grade ** slope) + 1 for grade in range(1, amount + 1)]
    largest = limit if full else min(limit, max(-(-total // amount), total * portions[0] // sum(portions)))
    least = 1 if total - largest >= amount - 1 else 0
    holding, surplus = [largest] + [least] * (amount - 1), total - largest - least * (amount - 1)
    while surplus > 0:
        candidates = [i for i in range(1, amount) if holding[i] < largest] or [i for i in range(1, amount) if holding[i] < limit]
        whole, left = sum([portions[i] for i in candidates]), surplus
        for i in candidates:
            more = min(limit - holding[i], max(1, left * portions[i] // whole), surplus)
            holding[i] = holding[i] + more
            surplus = surplus - more
    return np.array(holding)


def normal_values(key, shape, width, limit, cuts=(), dtype=jnp.bfloat16):
    entries = jax.random.normal(key, shape, jnp.float32) * width
    if len(cuts) > 0:
        entries = block_levels(key, shape, cuts, -0.22, 0.18) * entries
    return jnp.clip(entries, min=-limit, max=limit).astype(dtype)


def setup_inputs(seed: int = 0) -> dict:
    arg_keys = jax.random.split(jax.random.key(seed), 29)
    tokens = normal_values(arg_keys[0], (ROWS, ROW_LEN, D), 1.0, 6.0, ((0, 8), (1, 4)))
    seg_flags = draw_seg_flags(jax.random.fold_in(arg_keys[28], 71), 0)
    routes_keys = jax.random.split(jax.random.fold_in(arg_keys[2], 1), ROWS * ROW_LEN // TOK_DEV)
    routes_turns = jax.random.permutation(jax.random.fold_in(arg_keys[2], 3), ROWS * ROW_LEN // TOK_DEV)
    routes = jax.vmap(lambda own, number: assign_block(jax.random.fold_in(arg_keys[2], 2), own, number, TOK_DEV, EXPERTS, TOPK, CAP, 1))(routes_keys, routes_turns).reshape((ROWS, ROW_LEN, TOPK))
    out_grad = normal_values(arg_keys[3], (ROWS, ROW_LEN, D), 1.0, 6.0, ((0, 8), (1, 4)))
    w_in = normal_values(arg_keys[4], (D, PROJ), D ** -0.5, 0.15625, ((0, 32),), jnp.float32)
    w_in_m = normal_values(arg_keys[5], (D, PROJ), (0.044 * TOKENS_ALL ** 0.5), 24.0, ((0, 32),), jnp.float32)
    w_in_v = jnp.clip(jnp.exp(math.log(278.528) - 1.3981289 * jax.random.uniform(arg_keys[6], (D, PROJ), jnp.float32) ** block_levels(arg_keys[6], (D, PROJ), ((0, 32),), -0.2, 0.2)), 68.8128, 278.528)
    w_router = normal_values(arg_keys[7], (D, EXPERTS), (4 * D) ** -0.5, 0.078125, ((0, 32),), jnp.float32)
    w_router_m = normal_values(arg_keys[8], (D, EXPERTS), (1.1 * (TOKENS_ALL * TOPK // EXPERTS) ** 0.5), 384.0, ((0, 32),), jnp.float32)
    w_router_v = jnp.clip(jnp.exp(math.log(64512.0) - 1.37681564 * jax.random.uniform(arg_keys[9], (D, EXPERTS), jnp.float32) ** block_levels(arg_keys[9], (D, EXPERTS), ((0, 32),), -0.2, 0.2)), 16281.6, 64512.0)
    w_shared_in = normal_values(arg_keys[10], (D, 2 * SF), D ** -0.5, 0.15625, ((0, 32),), jnp.float32)
    w_shared_in_m = normal_values(arg_keys[11], (D, 2 * SF), (0.067 * TOKENS_ALL ** 0.5), 32.0, ((0, 32),), jnp.float32)
    w_shared_in_v = jnp.clip(jnp.exp(math.log(622.592) - 1.3862944 * jax.random.uniform(arg_keys[12], (D, 2 * SF), jnp.float32) ** block_levels(arg_keys[12], (D, 2 * SF), ((0, 32),), -0.2, 0.2)), 155.648, 622.592)
    w_out = normal_values(arg_keys[13], (DI, D), DI ** -0.5, 0.109375, ((0, 32),), jnp.float32)
    w_out_m = normal_values(arg_keys[14], (DI, D), (0.13 * TOKENS_ALL ** 0.5), 64.0, ((0, 32),), jnp.float32)
    w_out_v = jnp.clip(jnp.exp(math.log(2457.6) - 1.3730492 * jax.random.uniform(arg_keys[15], (DI, D), jnp.float32) ** block_levels(arg_keys[15], (DI, D), ((0, 32),), -0.2, 0.2)), 622.592, 2457.6)
    w_shared_out = normal_values(arg_keys[16], (SF, D), SF ** -0.5, 0.1875, ((0, 32),), jnp.float32)
    w_shared_out_m = normal_values(arg_keys[17], (SF, D), (0.067 * TOKENS_ALL ** 0.5), 32.0, ((0, 32),), jnp.float32)
    w_shared_out_v = jnp.clip(jnp.exp(math.log(622.592) - 1.3862944 * jax.random.uniform(arg_keys[18], (SF, D), jnp.float32) ** block_levels(arg_keys[18], (SF, D), ((0, 32),), -0.2, 0.2)), 155.648, 622.592)
    w_experts_in = normal_values(arg_keys[19], (EXPERTS, D, 2 * EF), D ** -0.5, 0.15625, ((0, 8), (1, 4)), jnp.float32)
    w_experts_in_m = normal_values(arg_keys[20], (EXPERTS, D, 2 * EF), (0.047 * (TOKENS_ALL * TOPK // EXPERTS) ** 0.5), 16.0, ((0, 8), (1, 4)), jnp.float32)
    w_experts_in_v = jnp.clip(jnp.exp(math.log(113.664) - 1.3809036 * jax.random.uniform(arg_keys[21], (EXPERTS, D, 2 * EF), jnp.float32) ** block_levels(arg_keys[21], (EXPERTS, D, 2 * EF), ((0, 8), (1, 4)), -0.2, 0.2)), 28.5696, 113.664)
    w_experts_out = normal_values(arg_keys[22], (EXPERTS, EF, D), (EF // TOPK) ** -0.5, 0.625, ((0, 8), (1, 4)), jnp.float32)
    w_experts_out_m = normal_values(arg_keys[23], (EXPERTS, EF, D), (0.011 * (TOKENS_ALL * TOPK // EXPERTS) ** 0.5), 4.0, ((0, 8), (1, 4)), jnp.float32)
    w_experts_out_v = jnp.clip(jnp.exp(math.log(6.4512) - 1.37681562 * jax.random.uniform(arg_keys[24], (EXPERTS, EF, D), jnp.float32) ** block_levels(arg_keys[24], (EXPERTS, EF, D), ((0, 8), (1, 4)), -0.2, 0.2)), 1.62816, 6.4512)
    small_params = draw_small_params(jax.random.fold_in(arg_keys[28], 71), 0)
    small_m = normal_values(arg_keys[26], (SMALL,), (0.056 * TOKENS_ALL ** 0.5), 32.0, (), jnp.float32)
    small_v = jnp.clip(jnp.exp(jax.random.uniform(arg_keys[27], (SMALL,), jnp.float32, math.log(106.496), math.log(434.176))), 106.496, 434.176)
    return {"tokens": tokens, "seg_flags": seg_flags, "routes": routes, "out_grad": out_grad, "w_in": w_in, "w_in_m": w_in_m, "w_in_v": w_in_v, "w_router": w_router, "w_router_m": w_router_m, "w_router_v": w_router_v, "w_shared_in": w_shared_in, "w_shared_in_m": w_shared_in_m, "w_shared_in_v": w_shared_in_v, "w_out": w_out, "w_out_m": w_out_m, "w_out_v": w_out_v, "w_shared_out": w_shared_out, "w_shared_out_m": w_shared_out_m, "w_shared_out_v": w_shared_out_v, "w_experts_in": w_experts_in, "w_experts_in_m": w_experts_in_m, "w_experts_in_v": w_experts_in_v, "w_experts_out": w_experts_out, "w_experts_out_m": w_experts_out_m, "w_experts_out_v": w_experts_out_v, "small_params": small_params, "small_m": small_m, "small_v": small_v}


EPS = 1e-05
BETA_ONE = 0.9
BETA_TWO = 0.95
ADAM_EPS = 1e-08
DECAY_RATE = 0.1
MATRIX_RATE = 0.4
SMALL_RATE = 0.2
HIGH = lax.Precision.HIGHEST
head_groups = 4

@jax.custom_vjp
def low(v):
    return lax.optimization_barrier(v.astype(jnp.bfloat16)).astype(jnp.float32)

@jax.custom_vjp
def low_back(v):
    return v

def low_keep(v):
    return (low(v), None)

def low_pass(kept, grad):
    return (grad,)

def back_keep(v):
    return (v, None)

def back_low(kept, grad):
    return (low(grad),)
low.defvjp(low_keep, low_pass)
low_back.defvjp(back_keep, back_low)

def unpack(small):
    widths = [D, KCONV * XBC, XBC, HEADS, HEADS, HEADS, DI, D]
    pieces = []
    offset = 0
    for extent in widths:
        pieces.append(small[offset:offset + extent])
        offset = offset + extent
    gain_one, conv_flat, conv_bias, dt_bias, a_log, d_skip, gain_mix, gain_two = pieces
    return (gain_one, conv_flat.reshape(KCONV, XBC), conv_bias, dt_bias, a_log, d_skip, gain_mix, gain_two)

def norm_rows(values, gain):
    return values * lax.rsqrt(lax.optimization_barrier(jnp.mean(values * values, -1, keepdims=True)) + EPS) * gain

def swiglu(joined):
    middle = joined.shape[-1] // 2
    return jax.nn.silu(joined[..., :middle]) * joined[..., middle:]

def gate_values(logits, chosen):
    return jax.nn.softmax(jnp.take_along_axis(logits, chosen, 1), -1)

def convolve(padded, conv_weight, conv_bias, padded_ids):
    length = padded.shape[0] - KCONV + 1
    own_ids = padded_ids[KCONV - 1:]
    summed = conv_bias + jnp.zeros((length, padded.shape[1]), jnp.float32)
    for offset in range(KCONV):
        first_row = KCONV - 1 - offset
        valid_tap = (padded_ids[first_row:first_row + length] == own_ids).astype(jnp.float32)
        summed = summed + conv_weight[offset] * padded[first_row:first_row + length] * valid_tap[:, None]
    return summed

def prepare(padded, dt_raw, conv_weight, conv_bias, dt_bias, a_log, padded_ids):
    activated = jax.nn.silu(convolve(padded, conv_weight, conv_bias, padded_ids))
    inputs = activated[:, :DI]
    b_proj = activated[:, DI:DI + STATE]
    c_proj = activated[:, DI + STATE:]
    step_size = jax.nn.softplus(dt_raw + dt_bias)
    log_decay = -step_size * jnp.exp(a_log)
    return (inputs, b_proj, c_proj, step_size, log_decay)

def ssd_summary(inputs, b_proj, step_size, log_decay, block_ids):
    cumulative = jnp.cumsum(log_decay, 0)
    last_id = block_ids[-1]
    tail_decay = jnp.exp(cumulative[-1][None, :] - cumulative) * (block_ids == last_id).astype(jnp.float32)[:, None]
    weighted = inputs.reshape(-1, HEADS, HEAD_DIM) * (step_size * tail_decay)[:, :, None]
    states = jnp.einsum('shp,sn->hpn', weighted, b_proj, precision=HIGH)
    carried = jnp.exp(cumulative[-1]) * (last_id == 0).astype(jnp.float32)
    return (carried, states)

def ssd_output(inputs, b_proj, c_proj, step_size, log_decay, gate_raw, d_skip, gain_mix, state_in, block_ids):
    row_count = inputs.shape[0]
    heads_in = inputs.reshape(row_count, HEADS, HEAD_DIM)
    cumulative = jnp.cumsum(log_decay, 0)
    places = jnp.arange(row_count)
    causal = (block_ids[:, None] == block_ids[None, :]) & (places[:, None] >= places[None, :])
    scores = jnp.dot(c_proj, b_proj.T, precision=HIGH) * causal.astype(jnp.float32)
    weighted = heads_in * step_size[:, :, None]
    group_size = HEADS // head_groups

    def one_group(payload):
        group_log, group_in = payload
        log_gaps = group_log[:, None, :] - group_log[None, :, :]
        decays = jnp.exp(jnp.where(causal[:, :, None], log_gaps, 0.0)) * scores[:, :, None]
        return jnp.einsum('tsh,shp->thp', decays, group_in, precision=HIGH)
    grouped = lax.map(jax.checkpoint(one_group), (cumulative.reshape(row_count, head_groups, group_size).transpose(1, 0, 2), weighted.reshape(row_count, head_groups, group_size, HEAD_DIM).transpose(1, 0, 2, 3)))
    within = grouped.transpose(1, 0, 2, 3).reshape(row_count, HEADS, HEAD_DIM)
    entry = jnp.exp(cumulative) * (block_ids == 0).astype(jnp.float32)[:, None]
    carried_in = jnp.einsum('tn,hpn->thp', c_proj, state_in, precision=HIGH) * entry[:, :, None]
    mixed = (within + carried_in + heads_in * d_skip[None, :, None]).reshape(row_count, DI)
    return norm_rows(mixed * jax.nn.silu(gate_raw), gain_mix)

def matrix_rates():
    return (MATRIX_RATE * D ** (-0.5), MATRIX_RATE * (4 * D) ** (-0.5), MATRIX_RATE * D ** (-0.5), MATRIX_RATE * DI ** (-0.5), MATRIX_RATE * SF ** (-0.5), MATRIX_RATE * D ** (-0.5), MATRIX_RATE * (EF // TOPK) ** (-0.5))

def adamw(weight, grad, first, second, rate, decay):
    first_new = BETA_ONE * first + (1.0 - BETA_ONE) * grad
    second_new = BETA_TWO * second + (1.0 - BETA_TWO) * grad * grad
    first_hat = first_new / (1.0 - BETA_ONE ** STEP)
    second_hat = second_new / (1.0 - BETA_TWO ** STEP)
    weight_new = weight - rate * (first_hat / (jnp.sqrt(second_hat) + ADAM_EPS) + decay * weight)
    return (weight_new, first_new, second_new)

def layer_row(x_row, flags_row, routes_row, lowered):
    w_in, w_router, w_shared_in, w_out, w_shared_out, w_experts_in, w_experts_out, small = lowered
    gain_one, conv_weight, conv_bias, dt_bias, a_log, d_skip, gain_mix, gain_two = unpack(small)
    blocks = ROW_LEN // TOK_DEV
    normed = low(norm_rows(x_row, gain_one))
    projected = low_back(jnp.dot(normed, w_in, precision=HIGH))
    gate_raw = projected[:, :DI]
    conv_in = low(projected[:, DI:DI + XBC])
    dt_raw = projected[:, DI + XBC:]
    segment_ids = jnp.cumsum(flags_row).astype(jnp.int32)
    padded = jnp.concatenate([jnp.zeros((KCONV - 1, XBC), jnp.float32), conv_in], 0)
    padded_ids = jnp.concatenate([-jnp.ones((KCONV - 1,), jnp.int32), segment_ids], 0)
    inputs, b_proj, c_proj, step_size, log_decay = prepare(padded, dt_raw, conv_weight, conv_bias, dt_bias, a_log, padded_ids)
    block_ids = jnp.cumsum(flags_row.reshape(blocks, TOK_DEV), 1).astype(jnp.int32)

    def ssd_block(state, payload):
        block_in, block_b, block_c, block_step, block_log, block_gate, block_seg = payload
        normed_out = ssd_output(block_in, block_b, block_c, block_step, block_log, block_gate, d_skip, gain_mix, state, block_seg)
        carried, states = ssd_summary(block_in, block_b, block_step, block_log, block_seg)
        return (carried[:, None, None] * state + states, normed_out)
    payload = tuple((array_in.reshape((blocks, TOK_DEV) + array_in.shape[1:]) for array_in in (inputs, b_proj, c_proj, step_size, log_decay, gate_raw))) + (block_ids,)
    final_state, normed_blocks = lax.scan(jax.checkpoint(ssd_block), jnp.zeros((HEADS, HEAD_DIM, STATE), jnp.float32), payload)
    mixer_low = low(normed_blocks.reshape(ROW_LEN, DI))
    residual = x_row + low_back(jnp.dot(mixer_low, w_out, precision=HIGH))
    normed_two = low(norm_rows(residual, gain_two))
    logits = low_back(jnp.dot(normed_two, w_router, precision=HIGH))
    shared_pre = low_back(jnp.dot(normed_two, w_shared_in, precision=HIGH))
    shared_low = low(swiglu(shared_pre))
    shared_result = low_back(jnp.dot(shared_low, w_shared_out, precision=HIGH))
    gates = gate_values(logits, routes_row)
    block_routes = routes_row.reshape(blocks, TOK_DEV * TOPK)
    onehot = (block_routes[:, :, None] == jnp.arange(EXPERTS)[None, None, :]).astype(jnp.int32)
    earlier = jnp.cumsum(onehot, 1) - onehot
    slots = lax.optimization_barrier(jnp.sum(earlier * onehot, 2)).astype(jnp.int32)
    position = (block_routes * CAP + slots).astype(jnp.int32)
    token_of = (jnp.arange(TOK_DEV * TOPK)[None, :] // TOPK + jnp.arange(blocks)[:, None] * TOK_DEV).astype(jnp.int32)
    block_index = (jnp.arange(blocks)[:, None] + jnp.zeros((1, TOK_DEV * TOPK), jnp.int32)).astype(jnp.int32)
    source = jnp.zeros((blocks, EXPERTS * CAP), jnp.int32).at[block_index, position].set(token_of)
    filled = jnp.zeros((blocks, EXPERTS * CAP), jnp.float32).at[block_index, position].set(1.0)
    buffer = low_back(normed_two[source] * filled[:, :, None])
    per_expert = buffer.reshape(blocks, EXPERTS, CAP, D).transpose(1, 0, 2, 3)

    def expert_fn(payload):
        rows_in, weight_in, weight_out = payload
        joined = low_back(jnp.einsum('bcd,df->bcf', rows_in, weight_in, precision=HIGH))
        hidden = low(swiglu(joined))
        return low(low_back(jnp.einsum('bcf,fd->bcd', hidden, weight_out, precision=HIGH)))
    expert_result = lax.map(jax.checkpoint(expert_fn), (per_expert, w_experts_in, w_experts_out))
    flat_result = expert_result.transpose(1, 0, 2, 3).reshape(blocks * EXPERTS * CAP, D)
    global_position = (position + jnp.arange(blocks)[:, None] * (EXPERTS * CAP)).astype(jnp.int32)
    picked = flat_result[global_position.reshape(-1)].reshape(ROW_LEN, TOPK, D)
    moe_result = lax.optimization_barrier(jnp.sum(gates[:, :, None] * picked, 1))
    return residual + shared_result + moe_result

def reference(tokens, seg_flags, routes, out_grad, w_in, w_in_m, w_in_v, w_router, w_router_m, w_router_v, w_shared_in, w_shared_in_m, w_shared_in_v, w_out, w_out_m, w_out_v, w_shared_out, w_shared_out_m, w_shared_out_v, w_experts_in, w_experts_in_m, w_experts_in_v, w_experts_out, w_experts_out_m, w_experts_out_v, small_params, small_m, small_v):
    weights = (w_in, w_router, w_shared_in, w_out, w_shared_out, w_experts_in, w_experts_out, small_params)
    firsts = (w_in_m, w_router_m, w_shared_in_m, w_out_m, w_shared_out_m, w_experts_in_m, w_experts_out_m, small_m)
    seconds = (w_in_v, w_router_v, w_shared_in_v, w_out_v, w_shared_out_v, w_experts_in_v, w_experts_out_v, small_v)

    def forward(inputs_all, params):
        lowered = tuple((low(member) for member in params[:7])) + (params[7],)

        def one_row(payload):
            return layer_row(payload[0], payload[1], payload[2], lowered)
        return lax.map(jax.checkpoint(one_row), (inputs_all, seg_flags, routes))
    outputs, pullback = jax.vjp(forward, tokens.astype(jnp.float32), weights)
    input_grad, weight_grads = pullback(out_grad.astype(jnp.float32))
    results = [outputs.astype(jnp.bfloat16), input_grad]
    rates = matrix_rates()
    for member in range(7):
        new_weight, new_first, new_second = adamw(weights[member], weight_grads[member], firsts[member], seconds[member], rates[member], DECAY_RATE)
        results = results + [new_weight, new_first, new_second]
    new_weight, new_first, new_second = adamw(small_params, weight_grads[7], small_m, small_v, SMALL_RATE, 0.0)
    results = results + [new_weight, new_first, new_second]
    return (results[0], results[1], results[2], results[3], results[4], results[5], results[6], results[7], results[8], results[9], results[10], results[11], results[12], results[13], results[14], results[15], results[16], results[17], results[18], results[19], results[20], results[21], results[22], results[23], results[24], results[25])
```

```python
from functools import partial

import jax
import jax.numpy as jnp
from jax import lax
from jax.experimental import pallas as pl
from jax.experimental.pallas import tpu as pltpu
from jax.sharding import PartitionSpec as P

D = 1536
HEADS = 48
HEAD_DIM = 64
STATE = 128
KCONV = 4
EF = 512
SF = 1024
TOPK = 6
EXP_DEV = 2
STEP = 10
DI = 3072
XBC = 3328
LANES = 128
CHUNK = 256

EPS = 1e-05
BETA_ONE = 0.9
BETA_TWO = 0.95
ADAM_EPS = 1e-08
DECAY_RATE = 0.1
MATRIX_RATE = 0.4
SMALL_RATE = 0.2
HIGH = lax.Precision.HIGHEST
BF = jnp.bfloat16
F32 = jnp.float32
NT = (((1,), (1,)), ((), ()))
TN = (((0,), (0,)), ((), ()))


def unpack(small):
    widths = [D, KCONV * XBC, XBC, HEADS, HEADS, HEADS, DI, D]
    pieces = []
    offset = 0
    for extent in widths:
        pieces.append(small[offset : offset + extent])
        offset = offset + extent
    gain_one, conv_flat, conv_bias, dt_bias, a_log, d_skip, gain_mix, gain_two = pieces
    return (
        gain_one,
        conv_flat.reshape(KCONV, XBC),
        conv_bias,
        dt_bias,
        a_log,
        d_skip,
        gain_mix,
        gain_two,
    )


def dot(left, right):
    return jnp.dot(left, right, preferred_element_type=F32)


def dot_nt(left, right):
    return lax.dot_general(left, right, NT, preferred_element_type=F32)


def dot_tn(left, right):
    return lax.dot_general(left, right, TN, preferred_element_type=F32)


def softplus(v):
    return jnp.maximum(v, 0.0) + jnp.log1p(jnp.exp(-jnp.abs(v)))


def sigmoid(v):
    return 1.0 / (1.0 + jnp.exp(-v))


def split_two(v):
    upper = v.astype(BF)
    lower = (v - upper.astype(F32)).astype(BF)
    return upper, lower


def mixer_common(proj, halo, cols, rows, halo_cols, convp, headp, cl):
    q = proj.shape[0]
    cc = cl + 2 * STATE
    raw = proj[:, cl : cl + cc].astype(BF).astype(F32)
    before = halo[:, cl : cl + cc].astype(BF).astype(F32)
    padded = jnp.concatenate([before, raw], 0)
    pre = convp[KCONV : KCONV + 1, :] + jnp.zeros((q, cc), F32)
    taps = []
    for j in range(KCONV):
        tap = padded[8 - j : 8 - j + q] * cols[:, j : j + 1]
        taps.append(tap)
        pre = pre + convp[j : j + 1, :] * tap
    gate = sigmoid(pre)
    act = pre * gate
    b_low = act[:, cl : cl + STATE].astype(BF)
    c_low = act[:, cl + STATE :].astype(BF)
    dt = proj[:, cl + cc : cl + cc + LANES] + headp[0:1, :]
    step = softplus(dt)
    decay_log = step * headp[1:2, :]
    at_row = lax.broadcasted_iota(jnp.int32, (q, q), 0)
    at_col = lax.broadcasted_iota(jnp.int32, (q, q), 1)
    lower = (at_row >= at_col).astype(F32)
    cum = jnp.dot(lower, decay_log, preferred_element_type=F32, precision=HIGH)
    cum_t = cum.T
    id_col = cols[:, 4:5]
    id_row = rows[0:1, :]
    id_last = id_col[q - 1 : q, :]
    id_prev = halo_cols[7:8, 4:5]
    causal = (id_col == id_row) & (at_row >= at_col)
    cum_end = cum[q - 1 : q, :]
    entry = jnp.exp(cum) * (id_col == id_prev).astype(F32)
    tail = jnp.exp(cum_end - cum) * (id_col == id_last).astype(F32)
    carried = jnp.exp(cum_end) * (id_last == id_prev).astype(F32)
    scores = dot_nt(c_low, b_low)
    return dict(
        taps=taps, pre=pre, gate=gate, act=act, b=b_low, c=c_low, dt=dt, step=step,
        decay_log=decay_log, lower=lower, cum=cum, cum_t=cum_t, causal=causal,
        entry=entry, tail=tail, carried=carried, scores=scores,
    )


def pair_lanes(values, first, is_left):
    return jnp.where(is_left, values[:, first : first + 1], values[:, first + 1 : first + 2])


def head_decay(m, head):
    gaps = m["cum"][:, head : head + 1] - m["cum_t"][head : head + 1, :]
    return jnp.exp(jnp.where(m["causal"], gaps, -1e30))


def mixer_forward_kernel(
    cl, proj_ref, halo_ref, cols_ref, rows_ref, halo_cols_ref, convp_ref, headp_ref, chanp_ref,
    low_ref, square_ref, out_ref, states_ref, state,
):
    q = proj_ref.shape[0]
    pairs = cl // LANES

    @pl.when(pl.program_id(0) == 0)
    def _():
        state[...] = jnp.zeros_like(state)

    proj = proj_ref[...]
    m = mixer_common(
        proj, halo_ref[...], cols_ref[...], rows_ref[0], halo_cols_ref[...], convp_ref[...],
        headp_ref[...], cl,
    )
    is_left = lax.broadcasted_iota(jnp.int32, (q, LANES), 1) < HEAD_DIM
    top = lax.broadcasted_iota(jnp.int32, (LANES, LANES), 0) < HEAD_DIM
    square = jnp.zeros((q, 1), F32)
    for p in range(pairs):
        span = slice(p * LANES, (p + 1) * LANES)
        held = state[p]
        states_ref[0, p] = held
        inputs = m["act"][:, span]
        weighted = inputs * pair_lanes(m["step"], 2 * p, is_left)
        left = jnp.where(is_left, weighted, 0.0).astype(BF)
        right = jnp.where(is_left, 0.0, weighted).astype(BF)
        mix_left = (m["scores"] * head_decay(m, 2 * p)).astype(BF)
        mix_right = (m["scores"] * head_decay(m, 2 * p + 1)).astype(BF)
        out = dot(mix_left, left) + dot(mix_right, right)
        out = out + dot_nt(m["c"], held.astype(BF)) * pair_lanes(m["entry"], 2 * p, is_left)
        out = out + chanp_ref[0:1, span] * inputs
        tailed = (weighted * pair_lanes(m["tail"], 2 * p, is_left)).astype(BF)
        kept = jnp.where(top, m["carried"][:, 2 * p : 2 * p + 1], m["carried"][:, 2 * p + 1 : 2 * p + 2])
        state[p] = kept * held + dot_tn(tailed, m["b"])
        z = proj[:, span]
        gated = out * (z * sigmoid(z))
        out_ref[:, span] = out
        low_ref[:, span] = (gated * chanp_ref[1:2, span]).astype(BF)
        square = square + jnp.sum(gated * gated, 1, keepdims=True)
    square_ref[...] = jnp.broadcast_to(square, (q, LANES))


def mixer_backward_kernel(
    cl, proj_ref, halo_ref, cols_ref, rows_ref, halo_cols_ref, convp_ref, headp_ref, chanp_ref,
    out_ref, states_ref, dmix_ref,
    dproj_ref, mlow_ref, dconv_ref, dhead_ref, dchan_ref,
    dstate, ends, dpre_next,
):
    q = proj_ref.shape[0]
    pairs = cl // LANES
    cc = cl + 2 * STATE

    @pl.when(pl.program_id(0) == 0)
    def _():
        dstate[...] = jnp.zeros_like(dstate)
        ends[...] = jnp.zeros_like(ends)
        dpre_next[...] = jnp.zeros_like(dpre_next)
        dconv_ref[...] = jnp.zeros_like(dconv_ref)
        dhead_ref[...] = jnp.zeros_like(dhead_ref)
        dchan_ref[...] = jnp.zeros_like(dchan_ref)

    proj = proj_ref[...]
    cols = cols_ref[...]
    convp = convp_ref[...]
    headp = headp_ref[...]
    m = mixer_common(
        proj, halo_ref[...], cols, rows_ref[0], halo_cols_ref[...], convp, headp, cl
    )
    root = cols[:, 5:6]
    along = cols[:, 6:7] * (root * root * root) * (1.0 / DI)
    is_left = lax.broadcasted_iota(jnp.int32, (q, LANES), 1) < HEAD_DIM
    top = lax.broadcasted_iota(jnp.int32, (LANES, LANES), 0) < HEAD_DIM
    lane = lax.broadcasted_iota(jnp.int32, (1, LANES), 1)
    dscores = jnp.zeros((q, q), F32)
    d_c = jnp.zeros((q, STATE), F32)
    d_b = jnp.zeros((q, STATE), F32)
    gap_grad = jnp.zeros((q, LANES), F32)
    step_grad = jnp.zeros((q, LANES), F32)
    next_ends = jnp.zeros((1, LANES), F32)
    d_act = []
    for p in range(pairs):
        span = slice(p * LANES, (p + 1) * LANES)
        held = states_ref[0, p]
        held_low = held.astype(BF)
        after = dstate[p]
        after_low = after.astype(BF)
        inputs = m["act"][:, span]
        step_p = pair_lanes(m["step"], 2 * p, is_left)
        entry_p = pair_lanes(m["entry"], 2 * p, is_left)
        tail_p = pair_lanes(m["tail"], 2 * p, is_left)
        weighted = inputs * step_p
        w_low = weighted.astype(BF)
        z = proj[:, span]
        sig = sigmoid(z)
        silu = z * sig
        out = out_ref[:, span]
        gated = out * silu
        dmix = dmix_ref[:, span].astype(F32)
        gain = chanp_ref[1:2, span]
        mlow_ref[:, span] = (gated * gain * root).astype(BF)
        dchan_ref[1:2, span] += jnp.sum(gated * root * dmix, 0, keepdims=True)
        dgated = root * gain * dmix - gated * along
        d_out = dgated * silu
        dproj_ref[:, span] = (dgated * out * (sig * (1.0 + z * (1.0 - sig)))).astype(BF)
        dchan_ref[0:1, span] += jnp.sum(d_out * inputs, 0, keepdims=True)
        skip = chanp_ref[0:1, span]
        d_left = jnp.where(is_left, d_out, 0.0).astype(BF)
        d_right = jnp.where(is_left, 0.0, d_out).astype(BF)
        decay_left = head_decay(m, 2 * p)
        decay_right = head_decay(m, 2 * p + 1)
        mix_left = (m["scores"] * decay_left).astype(BF)
        mix_right = (m["scores"] * decay_right).astype(BF)
        d_weighted = dot_tn(mix_left, d_left) + dot_tn(mix_right, d_right)
        d_weighted = d_weighted + tail_p * dot_nt(m["b"], after_low)
        dscores = dscores + dot_nt(d_left, w_low) * decay_left + dot_nt(d_right, w_low) * decay_right
        d_entered = (entry_p * d_out).astype(BF)
        d_c = d_c + dot(d_entered, held_low)
        d_b = d_b + dot((weighted * tail_p).astype(BF), after_low)
        kept = jnp.where(top, m["carried"][:, 2 * p : 2 * p + 1], m["carried"][:, 2 * p + 1 : 2 * p + 2])
        before = kept * after + dot_tn(d_entered, m["c"])
        dstate[p] = before
        product = jnp.sum(before * held, 1, keepdims=True)
        end_left = jnp.sum(product[:HEAD_DIM], 0, keepdims=True)
        end_right = jnp.sum(product[HEAD_DIM:], 0, keepdims=True)
        next_ends = next_ends + jnp.where(lane == 2 * p, end_left, 0.0)
        next_ends = next_ends + jnp.where(lane == 2 * p + 1, end_right, 0.0)
        d_act.append(d_weighted * step_p + skip * d_out)
        through = d_out * (out - skip * inputs) - weighted * d_weighted
        for side in range(2):
            pick = is_left if side == 0 else jnp.logical_not(is_left)
            here = lane == 2 * p + side
            gap_grad = gap_grad + jnp.where(
                here, jnp.sum(jnp.where(pick, through, 0.0), 1, keepdims=True), 0.0
            )
            step_grad = step_grad + jnp.where(
                here, jnp.sum(jnp.where(pick, d_weighted * inputs, 0.0), 1, keepdims=True), 0.0
            )
    ds_low = dscores.astype(BF) if False else jnp.where(m["causal"], dscores, 0.0).astype(BF)
    d_c = d_c + dot(ds_low, m["b"])
    d_b = d_b + dot_tn(ds_low, m["c"])
    last = lax.broadcasted_iota(jnp.int32, (q, LANES), 0) == q - 1
    gap_grad = gap_grad + jnp.where(last, ends[0:1, :], 0.0)
    ends[0:1, :] = next_ends
    d_log = lax.dot_general(
        m["lower"], gap_grad, TN, preferred_element_type=F32, precision=HIGH
    )
    d_dt = (step_grad + d_log * headp[1:2, :]) * sigmoid(m["dt"])
    d_dt = jnp.where(lane < 2 * pairs, d_dt, 0.0)
    dhead_ref[0:1, :] += jnp.sum(d_dt, 0, keepdims=True)
    dhead_ref[1:2, :] += jnp.sum(d_log * m["decay_log"], 0, keepdims=True)
    dproj_ref[:, cl + cc : cl + cc + LANES] = d_dt.astype(BF)
    d_pre = jnp.concatenate(d_act + [d_b, d_c], 1)
    gate = m["gate"]
    d_pre = d_pre * (gate * (1.0 + m["pre"] * (1.0 - gate)))
    dconv_ref[KCONV : KCONV + 1, :] += jnp.sum(d_pre, 0, keepdims=True)
    d_raw = jnp.zeros((q, cc), F32)
    for j in range(KCONV):
        dconv_ref[j : j + 1, :] += jnp.sum(d_pre * m["taps"][j], 0, keepdims=True)
        spread = d_pre * (convp[j : j + 1, :] * cols[:, j : j + 1])
        if j == 0:
            d_raw = d_raw + spread
        else:
            joined = jnp.concatenate([spread, dpre_next[j]], 0)
            d_raw = d_raw + joined[j : j + q]
            dpre_next[j] = spread[:8]
    dproj_ref[:, cl : cl + cc] = d_raw.astype(BF)


def mixer_specs(width, cl, chunks, order):
    cc = cl + 2 * STATE
    halo = CHUNK // 8

    def before(i):
        return (jnp.maximum(order(i) * halo - 1, 0), 0)

    return [
        pl.BlockSpec((CHUNK, width), lambda i: (order(i), 0)),
        pl.BlockSpec((8, width), before),
        pl.BlockSpec((CHUNK, LANES), lambda i: (order(i), 0)),
        pl.BlockSpec((1, 8, CHUNK), lambda i: (order(i), 0, 0)),
        pl.BlockSpec((8, LANES), before),
        pl.BlockSpec((8, cc), lambda i: (0, 0)),
        pl.BlockSpec((8, LANES), lambda i: (0, 0)),
        pl.BlockSpec((8, cl), lambda i: (0, 0)),
    ]


def mixer_forward(projected, cols, rows, convp, headp, chanp):
    length, width = projected.shape
    cl = chanp.shape[1]
    chunks = length // CHUNK
    pairs = cl // LANES
    return pl.pallas_call(
        partial(mixer_forward_kernel, cl),
        grid=(chunks,),
        in_specs=mixer_specs(width, cl, chunks, lambda i: i),
        out_specs=[
            pl.BlockSpec((CHUNK, cl), lambda i: (i, 0)),
            pl.BlockSpec((CHUNK, LANES), lambda i: (i, 0)),
            pl.BlockSpec((CHUNK, cl), lambda i: (i, 0)),
            pl.BlockSpec((1, pairs, LANES, STATE), lambda i: (i, 0, 0, 0)),
        ],
        out_shape=[
            jax.ShapeDtypeStruct((length, cl), BF),
            jax.ShapeDtypeStruct((length, LANES), F32),
            jax.ShapeDtypeStruct((length, cl), F32),
            jax.ShapeDtypeStruct((chunks, pairs, LANES, STATE), F32),
        ],
        scratch_shapes=[pltpu.VMEM((pairs, LANES, STATE), F32)],
        compiler_params=pltpu.CompilerParams(vmem_limit_bytes=56 * 2**20),
        name="mixer_forward",
    )(projected, projected, cols, rows, cols, convp, headp, chanp)


def mixer_backward(projected, cols, rows, convp, headp, chanp, out, states, dmix):
    length, width = projected.shape
    cl = chanp.shape[1]
    cc = cl + 2 * STATE
    chunks = length // CHUNK
    pairs = cl // LANES

    def order(i):
        return chunks - 1 - i

    return pl.pallas_call(
        partial(mixer_backward_kernel, cl),
        grid=(chunks,),
        in_specs=mixer_specs(width, cl, chunks, order)
        + [
            pl.BlockSpec((CHUNK, cl), lambda i: (order(i), 0)),
            pl.BlockSpec((1, pairs, LANES, STATE), lambda i: (order(i), 0, 0, 0)),
            pl.BlockSpec((CHUNK, cl), lambda i: (order(i), 0)),
        ],
        out_specs=[
            pl.BlockSpec((CHUNK, width), lambda i: (order(i), 0)),
            pl.BlockSpec((CHUNK, cl), lambda i: (order(i), 0)),
            pl.BlockSpec((8, cc), lambda i: (0, 0)),
            pl.BlockSpec((8, LANES), lambda i: (0, 0)),
            pl.BlockSpec((8, cl), lambda i: (0, 0)),
        ],
        out_shape=[
            jax.ShapeDtypeStruct((length, width), BF),
            jax.ShapeDtypeStruct((length, cl), BF),
            jax.ShapeDtypeStruct((8, cc), F32),
            jax.ShapeDtypeStruct((8, LANES), F32),
            jax.ShapeDtypeStruct((8, cl), F32),
        ],
        scratch_shapes=[
            pltpu.VMEM((pairs, LANES, STATE), F32),
            pltpu.VMEM((8, LANES), F32),
            pltpu.VMEM((KCONV, 8, cc), F32),
        ],
        compiler_params=pltpu.CompilerParams(vmem_limit_bytes=56 * 2**20),
        name="mixer_backward",
    )(projected, projected, cols, rows, cols, convp, headp, chanp, out, states, dmix)


def pad_rows(pieces, rows=8):
    stacked = jnp.stack(pieces, 0)
    return jnp.pad(stacked, ((0, rows - stacked.shape[0]), (0, 0)))


def pad_lanes(v, width=LANES):
    return jnp.pad(v, ((0, 0),) * (v.ndim - 1) + ((0, width - v.shape[-1]),))


def matrix_rates():
    return (
        MATRIX_RATE * D ** (-0.5),
        MATRIX_RATE * (4 * D) ** (-0.5),
        MATRIX_RATE * D ** (-0.5),
        MATRIX_RATE * DI ** (-0.5),
        MATRIX_RATE * SF ** (-0.5),
        MATRIX_RATE * D ** (-0.5),
        MATRIX_RATE * (EF // TOPK) ** (-0.5),
    )


def adamw(weight, grad, first, second, rate, decay):
    first_new = BETA_ONE * first + (1.0 - BETA_ONE) * grad
    second_new = BETA_TWO * second + (1.0 - BETA_TWO) * grad * grad
    first_hat = first_new / (1.0 - BETA_ONE**STEP)
    second_hat = second_new / (1.0 - BETA_TWO**STEP)
    weight_new = weight - rate * (first_hat / (jnp.sqrt(second_hat) + ADAM_EPS) + decay * weight)
    return (weight_new, first_new, second_new)


def gather_rows(v, axis):
    return lax.all_gather(v, axis, axis=0, tiled=True)


def scatter_rows(v, axis):
    return lax.psum_scatter(v, axis, scatter_dimension=0, tiled=True)


def swap_blocks(v, axis):
    return lax.all_to_all(v, axis, split_axis=0, concat_axis=0, tiled=True)


def masked_gates(logits, mask):
    highest = jnp.max(jnp.where(mask > 0, logits, -jnp.inf), -1, keepdims=True)
    raised = jnp.where(mask > 0, jnp.exp(logits - highest), 0.0)
    return raised / jnp.sum(raised, -1, keepdims=True)


def on_device(
    tokens,
    seg_flags,
    routes,
    out_grad,
    w_in,
    w_in_m,
    w_in_v,
    w_router,
    w_router_m,
    w_router_v,
    w_shared_in,
    w_shared_in_m,
    w_shared_in_v,
    w_out,
    w_out_m,
    w_out_v,
    w_shared_out,
    w_shared_out_m,
    w_shared_out_v,
    w_experts_in,
    w_experts_in_m,
    w_experts_in_v,
    w_experts_out,
    w_experts_out_m,
    w_experts_out_v,
    small_params,
    small_m,
    small_v,
):
    n_seq = lax.axis_size("seq")
    n_dp = lax.axis_size("dp")
    at_seq = lax.axis_index("seq")
    at_dp = lax.axis_index("dp")
    experts = EXP_DEV * n_dp
    length = seg_flags.shape[1]
    hl = HEADS // n_seq
    cl = hl * HEAD_DIM
    cc = cl + 2 * STATE
    rows_in = w_in.shape[0]
    rows_out = w_out.shape[0]
    shared_rows = w_shared_out.shape[0]
    x_local = tokens[0].astype(F32)
    cotangent = out_grad[0].astype(F32)
    gain_one, conv_weight, conv_bias, dt_bias, a_log, d_skip, gain_mix, gain_two = unpack(
        small_params
    )

    low_in = w_in.astype(BF)
    gate_part = low_in[:, :DI].reshape(rows_in, n_seq, cl)
    conv_part = low_in[:, DI : 2 * DI].reshape(rows_in, n_seq, cl)
    both_part = low_in[:, 2 * DI : 2 * DI + 2 * STATE]
    step_part = low_in[:, DI + XBC :].reshape(rows_in, n_seq, hl)
    tail_part = pad_lanes(
        jnp.concatenate(
            [step_part, jnp.broadcast_to(w_router.astype(BF)[:, None, :], (rows_in, n_seq, experts))],
            2,
        )
    )
    width = 2 * cl + 2 * STATE + LANES
    in_blocks = jnp.concatenate(
        [
            gate_part,
            conv_part,
            jnp.broadcast_to(both_part[:, None, :], (rows_in, n_seq, 2 * STATE)),
            tail_part,
        ],
        2,
    ).transpose(1, 0, 2)
    in_rows = swap_blocks(in_blocks, "seq")
    in_full = gather_rows(in_rows[None], "dp").transpose(1, 0, 2, 3).reshape(D, width)
    router = in_full[:, 2 * cl + 2 * STATE + hl : 2 * cl + 2 * STATE + hl + experts]
    out_full = gather_rows(w_out.astype(BF), "dp")

    mask = jnp.sum(
        (routes[0][:, :, None] == jnp.arange(experts)[None, None, :]).astype(F32), 1
    )
    cot_all = gather_rows(
        jnp.concatenate([out_grad[0], pad_lanes(mask.astype(BF))], 1), "dp"
    )
    mask_all = cot_all[:, D : D + experts].astype(F32)
    cot_all = cot_all[:, :D]

    shared_blocks = (
        w_shared_in.astype(BF)
        .reshape(rows_in, 2, n_seq, n_dp, shared_rows)
        .transpose(3, 0, 1, 2, 4)
        .reshape(n_dp, rows_in, 2 * n_seq * shared_rows)
    )
    sw = n_seq * shared_rows
    shared_cols = swap_blocks(shared_blocks, "dp").reshape(n_dp * rows_in, 2 * sw)
    e_low = w_experts_in.astype(BF)
    up_full = gather_rows(
        jnp.concatenate(
            [
                e_low[0, :, :EF], e_low[1, :, :EF], shared_cols[:, :sw],
                e_low[0, :, EF:], e_low[1, :, EF:], shared_cols[:, sw:],
            ],
            1,
        ),
        "seq",
    )
    hw = 2 * EF + sw
    ef_rows = w_experts_out.shape[1]
    down = gather_rows(
        jnp.concatenate(
            [w_experts_out[0].astype(BF), w_experts_out[1].astype(BF), w_shared_out.astype(BF)], 0
        )[None],
        "seq",
    )
    down_full = jnp.concatenate(
        [
            down[:, :ef_rows].reshape(EF, D),
            down[:, ef_rows : 2 * ef_rows].reshape(EF, D),
            down[:, 2 * ef_rows :].reshape(sw, D),
        ],
        0,
    )

    root_one = lax.rsqrt(jnp.mean(x_local * x_local, -1, keepdims=True) + EPS)
    normed_low = (x_local * root_one * gain_one).astype(BF)
    normed_all = gather_rows(normed_low, "seq")
    projected = dot(normed_all, in_full)
    ids = jnp.cumsum(seg_flags[0])
    ids_behind = [
        jnp.concatenate([-jnp.ones((j,), ids.dtype), ids[: length - j]], 0) for j in range(KCONV)
    ]
    valid = [(behind == ids).astype(F32) for behind in ids_behind]
    cols = pad_lanes(jnp.stack(valid + [ids.astype(F32)], 1))
    rows = jnp.broadcast_to(
        ids.astype(F32).reshape(length // CHUNK, 1, CHUNK), (length // CHUNK, 8, CHUNK)
    )

    def local_channels(v):
        mine = lax.dynamic_slice_in_dim(v, at_seq * cl, cl, v.ndim - 1)
        return jnp.concatenate([mine, v[..., DI:]], -1)

    def local_heads(v):
        return lax.dynamic_slice_in_dim(v, at_seq * hl, hl)

    convp = jnp.pad(
        jnp.concatenate([local_channels(conv_weight), local_channels(conv_bias)[None]], 0),
        ((0, 8 - KCONV - 1), (0, 0)),
    )
    a_own = -jnp.exp(local_heads(a_log))
    headp = pad_rows([pad_lanes(local_heads(dt_bias)), pad_lanes(a_own)])
    chanp = pad_rows(
        [
            jnp.repeat(local_heads(d_skip), HEAD_DIM),
            lax.dynamic_slice_in_dim(gain_mix, at_seq * cl, cl),
        ]
    )
    gated_low, squares, mixer_out, states = mixer_forward(projected, cols, rows, convp, headp, chanp)
    mixed = scatter_rows(
        jnp.concatenate(
            [dot(gated_low, out_full).astype(BF), pad_lanes(jnp.stack(split_two(squares[:, 0]), 1))],
            1,
        ),
        "seq",
    ).astype(F32)
    square_sum = mixed[:, D : D + 1] + mixed[:, D + 1 : D + 2]
    mixed = mixed[:, :D]
    root_mix = lax.rsqrt(square_sum / DI + EPS)
    residual = x_local + root_mix * mixed
    root_two = lax.rsqrt(jnp.mean(residual * residual, -1, keepdims=True) + EPS)
    normed_two_low = (residual * root_two * gain_two).astype(BF)

    two_all = gather_rows(normed_two_low, "dp")
    gates_all = masked_gates(dot(two_all, router), mask_all)
    gates_own = lax.dynamic_slice_in_dim(gates_all, at_dp * EXP_DEV, EXP_DEV, 1)
    spread = jnp.concatenate(
        [
            jnp.broadcast_to(gates_own[:, 0:1], (gates_own.shape[0], EF)),
            jnp.broadcast_to(gates_own[:, 1:2], (gates_own.shape[0], EF)),
            jnp.ones((gates_own.shape[0], sw), F32),
        ],
        1,
    )
    joined = dot(two_all, up_full)
    gate_half, up_half = joined[:, :hw], joined[:, hw:]
    sig = jax.nn.sigmoid(gate_half)
    silu = gate_half * sig
    hidden = (silu * up_half).astype(BF).astype(F32)
    hidden_gated = (hidden * spread).astype(BF)
    moe = scatter_rows(dot(hidden_gated, down_full).astype(BF), "dp")
    block_out = (residual + moe.astype(F32)).astype(BF)

    d_hidden = dot_nt(cot_all, down_full)
    touched = hidden * d_hidden
    d_gate_zero = jnp.sum(touched[:, :EF], 1)
    d_gate_one = jnp.sum(touched[:, EF : 2 * EF], 1)
    d_hidden = d_hidden * spread
    d_joined = jnp.concatenate(
        [d_hidden * up_half * (sig * (1.0 + gate_half * (1.0 - sig))), d_hidden * silu], 1
    ).astype(BF)
    grad_up = dot_tn(two_all, d_joined)
    grad_down = dot_tn(hidden_gated, cot_all)
    expert_place = jnp.arange(experts)[None, :]
    d_gates = jnp.where(expert_place == at_dp * EXP_DEV, d_gate_zero[:, None], 0.0) + jnp.where(
        expert_place == at_dp * EXP_DEV + 1, d_gate_one[:, None], 0.0
    )
    returned = scatter_rows(
        jnp.concatenate(
            [dot_nt(d_joined, up_full).astype(BF), pad_lanes(jnp.concatenate(split_two(d_gates), 1))],
            1,
        ),
        "dp",
    ).astype(F32)
    d_gates = returned[:, D : D + experts] + returned[:, D + experts : D + 2 * experts]
    gates = masked_gates(dot(normed_two_low, router), mask)
    d_logits = gates * (d_gates - jnp.sum(gates * d_gates, 1, keepdims=True))
    d_logits = d_logits.astype(BF)
    grad_router = dot_tn(normed_two_low, d_logits)
    d_normed_two = returned[:, :D] + dot_nt(d_logits, router)
    grad_gain_two = jnp.sum(d_normed_two * residual * root_two, 0)
    scaled = d_normed_two * gain_two
    d_residual = (
        cotangent
        + scaled * root_two
        - residual * (root_two**3 / D * jnp.sum(scaled * residual, -1, keepdims=True))
    )
    residual_low = d_residual.astype(BF)
    along = jnp.sum(residual_low.astype(F32) * mixed, 1)
    packed = jnp.stack(split_two(root_mix[:, 0]) + split_two(along), 1)
    residual_all = gather_rows(jnp.concatenate([residual_low, pad_lanes(packed)], 1), "seq")
    packed = residual_all[:, D : D + 4].astype(F32)
    residual_all = residual_all[:, :D]
    cols_back = jnp.concatenate(
        [cols[:, :5], packed[:, 0:1] + packed[:, 1:2], packed[:, 2:3] + packed[:, 3:4], cols[:, 7:]], 1
    )
    d_mixer = dot_nt(residual_all, out_full)
    d_proj, mixer_low, d_conv, d_head, d_chan = mixer_backward(
        projected, cols_back, rows, convp, headp, chanp, mixer_out, states, d_mixer
    )
    grad_out = dot_tn(mixer_low, residual_all)
    d_normed = scatter_rows(dot_nt(d_proj, in_full).astype(BF), "seq").astype(F32)
    grad_gain_one = jnp.sum(d_normed * x_local * root_one, 0)
    scaled = d_normed * gain_one
    input_grad = (
        d_residual
        + scaled * root_one
        - x_local * (root_one**3 / D * jnp.sum(scaled * x_local, -1, keepdims=True))
    )
    grad_in = dot_tn(normed_all, d_proj)
    first_router = 2 * cl + 2 * STATE + hl
    grad_in = grad_in + jnp.pad(grad_router, ((0, 0), (first_router, width - first_router - experts)))

    grad_in_rows = scatter_rows(
        grad_in.astype(BF).reshape(n_seq, n_dp, rows_in, width).transpose(1, 0, 2, 3), "dp"
    )[0]
    grad_in_own = swap_blocks(grad_in_rows, "seq").astype(F32)
    grad_w_in = jnp.concatenate(
        [
            grad_in_own[:, :, :cl].transpose(1, 0, 2).reshape(rows_in, DI),
            grad_in_own[:, :, cl : 2 * cl].transpose(1, 0, 2).reshape(rows_in, DI),
            jnp.sum(grad_in_own[:, :, 2 * cl : 2 * cl + 2 * STATE], 0),
            grad_in_own[:, :, 2 * cl + 2 * STATE : first_router].transpose(1, 0, 2).reshape(rows_in, HEADS),
        ],
        1,
    )
    grad_w_router = jnp.sum(grad_in_own[:, :, first_router : first_router + experts], 0)
    grad_w_out = scatter_rows(grad_out.astype(BF), "dp").astype(F32)
    grad_up = scatter_rows(grad_up.astype(BF), "seq")
    grad_shared_cols = jnp.concatenate([grad_up[:, 2 * EF : hw], grad_up[:, hw + 2 * EF :]], 1)
    grad_w_shared_in = (
        swap_blocks(grad_shared_cols.reshape(n_dp, rows_in, 2 * sw), "dp")
        .astype(F32)
        .reshape(n_dp, rows_in, 2, n_seq, shared_rows)
        .transpose(1, 2, 3, 0, 4)
        .reshape(rows_in, 2 * SF)
    )
    grad_up = grad_up.astype(F32)
    grad_w_experts_in = jnp.stack(
        [
            jnp.concatenate([grad_up[:, :EF], grad_up[:, hw : hw + EF]], 1),
            jnp.concatenate([grad_up[:, EF : 2 * EF], grad_up[:, hw + EF : hw + 2 * EF]], 1),
        ],
        0,
    )
    grad_down = scatter_rows(
        jnp.concatenate(
            [
                grad_down[:EF].reshape(n_seq, ef_rows, D),
                grad_down[EF : 2 * EF].reshape(n_seq, ef_rows, D),
                grad_down[2 * EF :].reshape(n_seq, shared_rows, D),
            ],
            1,
        ).astype(BF),
        "seq",
    )[0].astype(F32)
    grad_w_experts_out = grad_down[: 2 * ef_rows].reshape(2, ef_rows, D)
    grad_w_shared_out = grad_down[2 * ef_rows :]

    def place_channels(v):
        base = jnp.zeros(v.shape[:-1] + (XBC,), F32)
        base = lax.dynamic_update_slice_in_dim(base, v[..., :cl], at_seq * cl, v.ndim - 1)
        return lax.dynamic_update_slice_in_dim(base, v[..., cl:], DI, v.ndim - 1)

    def place(v, whole):
        return lax.dynamic_update_slice_in_dim(
            jnp.zeros((whole,), F32), v, at_seq * v.shape[0], 0
        )

    small_local = jnp.concatenate(
        [
            grad_gain_one,
            place_channels(d_conv[:KCONV]).reshape(-1),
            place_channels(d_conv[KCONV]),
            place(d_head[0, :hl], HEADS),
            place(d_head[1, :hl], HEADS),
            place(jnp.sum(d_chan[0].reshape(hl, HEAD_DIM), 1), HEADS),
            place(d_chan[1], DI),
            grad_gain_two,
        ],
        0,
    )
    small_grad = lax.psum(small_local, ("seq", "dp"))

    masters = (w_in, w_router, w_shared_in, w_out, w_shared_out, w_experts_in, w_experts_out)
    firsts = (
        w_in_m,
        w_router_m,
        w_shared_in_m,
        w_out_m,
        w_shared_out_m,
        w_experts_in_m,
        w_experts_out_m,
    )
    seconds = (
        w_in_v,
        w_router_v,
        w_shared_in_v,
        w_out_v,
        w_shared_out_v,
        w_experts_in_v,
        w_experts_out_v,
    )
    gradients = (
        grad_w_in,
        grad_w_router,
        grad_w_shared_in,
        grad_w_out,
        grad_w_shared_out,
        grad_w_experts_in,
        grad_w_experts_out,
    )
    rates = matrix_rates()
    results = [block_out[None], input_grad[None]]
    for member in range(7):
        results = results + list(
            adamw(
                masters[member],
                gradients[member],
                firsts[member],
                seconds[member],
                rates[member],
                DECAY_RATE,
            )
        )
    results = results + list(
        adamw(small_params, small_grad, small_m, small_v, SMALL_RATE, 0.0)
    )
    return tuple(results)


def solution(mesh):
    by_token = P("dp", "seq", None)
    dense = P(("seq", "dp"), None)
    expert = P("dp", "seq", None)
    weights = (dense,) * 15 + (expert,) * 6 + (P(),) * 3
    return jax.shard_map(
        on_device,
        mesh=mesh,
        in_specs=(by_token, P("dp", None), by_token, by_token) + weights,
        out_specs=(by_token, by_token) + weights,
        check_vma=False,
    )
```

```python
from functools import partial

import jax
import jax.numpy as jnp
from jax import lax
from jax.experimental import pallas as pl
from jax.experimental.pallas import tpu as pltpu
from jax.sharding import PartitionSpec as P

D = 1536
HEADS = 48
HEAD_DIM = 64
STATE = 128
KCONV = 4
EF = 512
SF = 1024
TOPK = 6
EXP_DEV = 2
STEP = 10
DI = 3072
XBC = 3328
LANES = 128
CHUNK = 256

EPS = 1e-05
BETA_ONE = 0.9
BETA_TWO = 0.95
ADAM_EPS = 1e-08
DECAY_RATE = 0.1
MATRIX_RATE = 0.4
SMALL_RATE = 0.2
HIGH = lax.Precision.HIGHEST
BF = jnp.bfloat16
F32 = jnp.float32
NT = (((1,), (1,)), ((), ()))
TN = (((0,), (0,)), ((), ()))


def unpack(small):
    widths = [D, KCONV * XBC, XBC, HEADS, HEADS, HEADS, DI, D]
    pieces = []
    offset = 0
    for extent in widths:
        pieces.append(small[offset : offset + extent])
        offset = offset + extent
    gain_one, conv_flat, conv_bias, dt_bias, a_log, d_skip, gain_mix, gain_two = pieces
    return (
        gain_one,
        conv_flat.reshape(KCONV, XBC),
        conv_bias,
        dt_bias,
        a_log,
        d_skip,
        gain_mix,
        gain_two,
    )


def dot(left, right):
    return jnp.dot(left, right, preferred_element_type=F32)


def dot_nt(left, right):
    return lax.dot_general(left, right, NT, preferred_element_type=F32)


def dot_tn(left, right):
    return lax.dot_general(left, right, TN, preferred_element_type=F32)


def softplus(v):
    return jnp.maximum(v, 0.0) + jnp.log1p(jnp.exp(-jnp.abs(v)))


def sigmoid(v):
    return 1.0 / (1.0 + jnp.exp(-v))


def split_two(v):
    upper = v.astype(BF)
    lower = (v - upper.astype(F32)).astype(BF)
    return upper, lower


def mixer_common(proj, halo, cols, rows, halo_cols, convp, headp, cl):
    q = proj.shape[0]
    cc = cl + 2 * STATE
    raw = proj[:, cl : cl + cc].astype(BF).astype(F32)
    before = halo[:, cl : cl + cc].astype(BF).astype(F32)
    padded = jnp.concatenate([before, raw], 0)
    pre = convp[KCONV : KCONV + 1, :] + jnp.zeros((q, cc), F32)
    taps = []
    for j in range(KCONV):
        tap = padded[8 - j : 8 - j + q] * cols[:, j : j + 1]
        taps.append(tap)
        pre = pre + convp[j : j + 1, :] * tap
    gate = sigmoid(pre)
    act = pre * gate
    b_low = act[:, cl : cl + STATE].astype(BF)
    c_low = act[:, cl + STATE :].astype(BF)
    dt = proj[:, cl + cc : cl + cc + LANES] + headp[0:1, :]
    step = softplus(dt)
    decay_log = step * headp[1:2, :]
    at_row = lax.broadcasted_iota(jnp.int32, (q, q), 0)
    at_col = lax.broadcasted_iota(jnp.int32, (q, q), 1)
    lower = (at_row >= at_col).astype(F32)
    cum = jnp.dot(lower, decay_log, preferred_element_type=F32, precision=HIGH)
    cum_t = cum.T
    id_col = cols[:, 4:5]
    id_row = rows[0:1, :]
    id_last = id_col[q - 1 : q, :]
    id_prev = halo_cols[7:8, 4:5]
    causal = (id_col == id_row) & (at_row >= at_col)
    cum_end = cum[q - 1 : q, :]
    entry = jnp.exp(cum) * (id_col == id_prev).astype(F32)
    tail = jnp.exp(cum_end - cum) * (id_col == id_last).astype(F32)
    carried = jnp.exp(cum_end) * (id_last == id_prev).astype(F32)
    scores = dot_nt(c_low, b_low)
    return dict(
        taps=taps, pre=pre, gate=gate, act=act, b=b_low, c=c_low, dt=dt, step=step,
        decay_log=decay_log, lower=lower, cum=cum, cum_t=cum_t, causal=causal,
        entry=entry, tail=tail, carried=carried, scores=scores,
    )


def pair_lanes(values, first, is_left):
    return jnp.where(is_left, values[:, first : first + 1], values[:, first + 1 : first + 2])


def head_decay(m, head):
    gaps = m["cum"][:, head : head + 1] - m["cum_t"][head : head + 1, :]
    return jnp.exp(jnp.where(m["causal"], gaps, -1e30))


def mixer_forward_kernel(
    cl, proj_ref, halo_ref, cols_ref, rows_ref, halo_cols_ref, convp_ref, headp_ref, chanp_ref,
    low_ref, square_ref, out_ref, states_ref, state,
):
    q = proj_ref.shape[0]
    pairs = cl // LANES

    @pl.when(pl.program_id(0) == 0)
    def _():
        state[...] = jnp.zeros_like(state)

    proj = proj_ref[...]
    m = mixer_common(
        proj, halo_ref[...], cols_ref[...], rows_ref[0], halo_cols_ref[...], convp_ref[...],
        headp_ref[...], cl,
    )
    is_left = lax.broadcasted_iota(jnp.int32, (q, LANES), 1) < HEAD_DIM
    top = lax.broadcasted_iota(jnp.int32, (LANES, LANES), 0) < HEAD_DIM
    square = jnp.zeros((q, 1), F32)
    for p in range(pairs):
        span = slice(p * LANES, (p + 1) * LANES)
        held = state[p]
        states_ref[0, p] = held
        inputs = m["act"][:, span]
        weighted = inputs * pair_lanes(m["step"], 2 * p, is_left)
        left = jnp.where(is_left, weighted, 0.0).astype(BF)
        right = jnp.where(is_left, 0.0, weighted).astype(BF)
        mix_left = (m["scores"] * head_decay(m, 2 * p)).astype(BF)
        mix_right = (m["scores"] * head_decay(m, 2 * p + 1)).astype(BF)
        out = dot(mix_left, left) + dot(mix_right, right)
        out = out + dot_nt(m["c"], held.astype(BF)) * pair_lanes(m["entry"], 2 * p, is_left)
        out = out + chanp_ref[0:1, span] * inputs
        tailed = (weighted * pair_lanes(m["tail"], 2 * p, is_left)).astype(BF)
        kept = jnp.where(top, m["carried"][:, 2 * p : 2 * p + 1], m["carried"][:, 2 * p + 1 : 2 * p + 2])
        state[p] = kept * held + dot_tn(tailed, m["b"])
        z = proj[:, span]
        gated = out * (z * sigmoid(z))
        out_ref[:, span] = out
        low_ref[:, span] = (gated * chanp_ref[1:2, span]).astype(BF)
        square = square + jnp.sum(gated * gated, 1, keepdims=True)
    square_ref[...] = jnp.broadcast_to(square, (q, LANES))


def mixer_backward_kernel(
    cl, proj_ref, halo_ref, cols_ref, rows_ref, halo_cols_ref, convp_ref, headp_ref, chanp_ref,
    out_ref, states_ref, dmix_ref,
    dproj_ref, mlow_ref, dconv_ref, dhead_ref, dchan_ref,
    dstate, ends, dpre_next,
):
    q = proj_ref.shape[0]
    pairs = cl // LANES
    cc = cl + 2 * STATE

    @pl.when(pl.program_id(0) == 0)
    def _():
        dstate[...] = jnp.zeros_like(dstate)
        ends[...] = jnp.zeros_like(ends)
        dpre_next[...] = jnp.zeros_like(dpre_next)
        dconv_ref[...] = jnp.zeros_like(dconv_ref)
        dhead_ref[...] = jnp.zeros_like(dhead_ref)
        dchan_ref[...] = jnp.zeros_like(dchan_ref)

    proj = proj_ref[...]
    cols = cols_ref[...]
    convp = convp_ref[...]
    headp = headp_ref[...]
    m = mixer_common(
        proj, halo_ref[...], cols, rows_ref[0], halo_cols_ref[...], convp, headp, cl
    )
    root = cols[:, 5:6]
    along = cols[:, 6:7] * (root * root * root) * (1.0 / DI)
    is_left = lax.broadcasted_iota(jnp.int32, (q, LANES), 1) < HEAD_DIM
    top = lax.broadcasted_iota(jnp.int32, (LANES, LANES), 0) < HEAD_DIM
    lane = lax.broadcasted_iota(jnp.int32, (1, LANES), 1)
    dscores = jnp.zeros((q, q), F32)
    d_c = jnp.zeros((q, STATE), F32)
    d_b = jnp.zeros((q, STATE), F32)
    gap_grad = jnp.zeros((q, LANES), F32)
    step_grad = jnp.zeros((q, LANES), F32)
    next_ends = jnp.zeros((1, LANES), F32)
    d_act = []
    for p in range(pairs):
        span = slice(p * LANES, (p + 1) * LANES)
        held = states_ref[0, p]
        held_low = held.astype(BF)
        after = dstate[p]
        after_low = after.astype(BF)
        inputs = m["act"][:, span]
        step_p = pair_lanes(m["step"], 2 * p, is_left)
        entry_p = pair_lanes(m["entry"], 2 * p, is_left)
        tail_p = pair_lanes(m["tail"], 2 * p, is_left)
        weighted = inputs * step_p
        w_low = weighted.astype(BF)
        z = proj[:, span]
        sig = sigmoid(z)
        silu = z * sig
        out = out_ref[:, span]
        gated = out * silu
        dmix = dmix_ref[:, span].astype(F32)
        gain = chanp_ref[1:2, span]
        mlow_ref[:, span] = (gated * gain * root).astype(BF)
        dchan_ref[1:2, span] += jnp.sum(gated * root * dmix, 0, keepdims=True)
        dgated = root * gain * dmix - gated * along
        d_out = dgated * silu
        dproj_ref[:, span] = (dgated * out * (sig * (1.0 + z * (1.0 - sig)))).astype(BF)
        dchan_ref[0:1, span] += jnp.sum(d_out * inputs, 0, keepdims=True)
        skip = chanp_ref[0:1, span]
        d_left = jnp.where(is_left, d_out, 0.0).astype(BF)
        d_right = jnp.where(is_left, 0.0, d_out).astype(BF)
        decay_left = head_decay(m, 2 * p)
        decay_right = head_decay(m, 2 * p + 1)
        mix_left = (m["scores"] * decay_left).astype(BF)
        mix_right = (m["scores"] * decay_right).astype(BF)
        d_weighted = dot_tn(mix_left, d_left) + dot_tn(mix_right, d_right)
        d_weighted = d_weighted + tail_p * dot_nt(m["b"], after_low)
        dscores = dscores + dot_nt(d_left, w_low) * decay_left + dot_nt(d_right, w_low) * decay_right
        d_entered = (entry_p * d_out).astype(BF)
        d_c = d_c + dot(d_entered, held_low)
        d_b = d_b + dot((weighted * tail_p).astype(BF), after_low)
        kept = jnp.where(top, m["carried"][:, 2 * p : 2 * p + 1], m["carried"][:, 2 * p + 1 : 2 * p + 2])
        before = kept * after + dot_tn(d_entered, m["c"])
        dstate[p] = before
        product = jnp.sum(before * held, 1, keepdims=True)
        end_left = jnp.sum(product[:HEAD_DIM], 0, keepdims=True)
        end_right = jnp.sum(product[HEAD_DIM:], 0, keepdims=True)
        next_ends = next_ends + jnp.where(lane == 2 * p, end_left, 0.0)
        next_ends = next_ends + jnp.where(lane == 2 * p + 1, end_right, 0.0)
        d_act.append(d_weighted * step_p + skip * d_out)
        through = d_out * (out - skip * inputs) - weighted * d_weighted
        for side in range(2):
            pick = is_left if side == 0 else jnp.logical_not(is_left)
            here = lane == 2 * p + side
            gap_grad = gap_grad + jnp.where(
                here, jnp.sum(jnp.where(pick, through, 0.0), 1, keepdims=True), 0.0
            )
            step_grad = step_grad + jnp.where(
                here, jnp.sum(jnp.where(pick, d_weighted * inputs, 0.0), 1, keepdims=True), 0.0
            )
    ds_low = dscores.astype(BF) if False else jnp.where(m["causal"], dscores, 0.0).astype(BF)
    d_c = d_c + dot(ds_low, m["b"])
    d_b = d_b + dot_tn(ds_low, m["c"])
    last = lax.broadcasted_iota(jnp.int32, (q, LANES), 0) == q - 1
    gap_grad = gap_grad + jnp.where(last, ends[0:1, :], 0.0)
    ends[0:1, :] = next_ends
    d_log = lax.dot_general(
        m["lower"], gap_grad, TN, preferred_element_type=F32, precision=HIGH
    )
    d_dt = (step_grad + d_log * headp[1:2, :]) * sigmoid(m["dt"])
    d_dt = jnp.where(lane < 2 * pairs, d_dt, 0.0)
    dhead_ref[0:1, :] += jnp.sum(d_dt, 0, keepdims=True)
    dhead_ref[1:2, :] += jnp.sum(d_log * m["decay_log"], 0, keepdims=True)
    dproj_ref[:, cl + cc : cl + cc + LANES] = d_dt.astype(BF)
    d_pre = jnp.concatenate(d_act + [d_b, d_c], 1)
    gate = m["gate"]
    d_pre = d_pre * (gate * (1.0 + m["pre"] * (1.0 - gate)))
    dconv_ref[KCONV : KCONV + 1, :] += jnp.sum(d_pre, 0, keepdims=True)
    d_raw = jnp.zeros((q, cc), F32)
    for j in range(KCONV):
        dconv_ref[j : j + 1, :] += jnp.sum(d_pre * m["taps"][j], 0, keepdims=True)
        spread = d_pre * (convp[j : j + 1, :] * cols[:, j : j + 1])
        if j == 0:
            d_raw = d_raw + spread
        else:
            joined = jnp.concatenate([spread, dpre_next[j]], 0)
            d_raw = d_raw + joined[j : j + q]
            dpre_next[j] = spread[:8]
    dproj_ref[:, cl : cl + cc] = d_raw.astype(BF)


def mixer_specs(width, cl, chunks, order):
    cc = cl + 2 * STATE
    halo = CHUNK // 8

    def before(i):
        return (jnp.maximum(order(i) * halo - 1, 0), 0)

    return [
        pl.BlockSpec((CHUNK, width), lambda i: (order(i), 0)),
        pl.BlockSpec((8, width), before),
        pl.BlockSpec((CHUNK, LANES), lambda i: (order(i), 0)),
        pl.BlockSpec((1, 8, CHUNK), lambda i: (order(i), 0, 0)),
        pl.BlockSpec((8, LANES), before),
        pl.BlockSpec((8, cc), lambda i: (0, 0)),
        pl.BlockSpec((8, LANES), lambda i: (0, 0)),
        pl.BlockSpec((8, cl), lambda i: (0, 0)),
    ]


def mixer_forward(projected, cols, rows, convp, headp, chanp):
    length, width = projected.shape
    cl = chanp.shape[1]
    chunks = length // CHUNK
    pairs = cl // LANES
    return pl.pallas_call(
        partial(mixer_forward_kernel, cl),
        grid=(chunks,),
        in_specs=mixer_specs(width, cl, chunks, lambda i: i),
        out_specs=[
            pl.BlockSpec((CHUNK, cl), lambda i: (i, 0)),
            pl.BlockSpec((CHUNK, LANES), lambda i: (i, 0)),
            pl.BlockSpec((CHUNK, cl), lambda i: (i, 0)),
            pl.BlockSpec((1, pairs, LANES, STATE), lambda i: (i, 0, 0, 0)),
        ],
        out_shape=[
            jax.ShapeDtypeStruct((length, cl), BF),
            jax.ShapeDtypeStruct((length, LANES), F32),
            jax.ShapeDtypeStruct((length, cl), F32),
            jax.ShapeDtypeStruct((chunks, pairs, LANES, STATE), F32),
        ],
        scratch_shapes=[pltpu.VMEM((pairs, LANES, STATE), F32)],
        compiler_params=pltpu.CompilerParams(vmem_limit_bytes=56 * 2**20),
        name="mixer_forward",
    )(projected, projected, cols, rows, cols, convp, headp, chanp)


def mixer_backward(projected, cols, rows, convp, headp, chanp, out, states, dmix):
    length, width = projected.shape
    cl = chanp.shape[1]
    cc = cl + 2 * STATE
    chunks = length // CHUNK
    pairs = cl // LANES

    def order(i):
        return chunks - 1 - i

    return pl.pallas_call(
        partial(mixer_backward_kernel, cl),
        grid=(chunks,),
        in_specs=mixer_specs(width, cl, chunks, order)
        + [
            pl.BlockSpec((CHUNK, cl), lambda i: (order(i), 0)),
            pl.BlockSpec((1, pairs, LANES, STATE), lambda i: (order(i), 0, 0, 0)),
            pl.BlockSpec((CHUNK, cl), lambda i: (order(i), 0)),
        ],
        out_specs=[
            pl.BlockSpec((CHUNK, width), lambda i: (order(i), 0)),
            pl.BlockSpec((CHUNK, cl), lambda i: (order(i), 0)),
            pl.BlockSpec((8, cc), lambda i: (0, 0)),
            pl.BlockSpec((8, LANES), lambda i: (0, 0)),
            pl.BlockSpec((8, cl), lambda i: (0, 0)),
        ],
        out_shape=[
            jax.ShapeDtypeStruct((length, width), BF),
            jax.ShapeDtypeStruct((length, cl), BF),
            jax.ShapeDtypeStruct((8, cc), F32),
            jax.ShapeDtypeStruct((8, LANES), F32),
            jax.ShapeDtypeStruct((8, cl), F32),
        ],
        scratch_shapes=[
            pltpu.VMEM((pairs, LANES, STATE), F32),
            pltpu.VMEM((8, LANES), F32),
            pltpu.VMEM((KCONV, 8, cc), F32),
        ],
        compiler_params=pltpu.CompilerParams(vmem_limit_bytes=56 * 2**20),
        name="mixer_backward",
    )(projected, projected, cols, rows, cols, convp, headp, chanp, out, states, dmix)


MESH = pl.DeviceIdType.MESH


def plane(axis):
    size = lax.axis_size(axis)
    fast = 2 if axis == "seq" else max(1, size // 4)
    return size // fast, fast


def place_in(axis):
    n_slow, n_fast = plane(axis)
    me = lax.axis_index(axis)
    return me, me // n_fast, me % n_fast


def greet(axes):
    barrier = pltpu.get_barrier_semaphore()
    count = 0
    for axis in axes:
        size = lax.axis_size(axis)
        me = lax.axis_index(axis)
        for away in range(1, size):
            pl.semaphore_signal(
                barrier, inc=1, device_id={axis: (me + away) % size}, device_id_type=MESH
            )
        count = count + size - 1
    pl.semaphore_wait(barrier, count)


class Exchange:
    def __init__(self, axis, src, dst, send, recv, local):
        self.axis, self.src, self.dst = axis, src, dst
        self.send, self.recv, self.local = send, recv, local
        self.size = lax.axis_size(axis)
        self.me = lax.axis_index(axis)

    @staticmethod
    def scratch(axis):
        size = lax.axis_size(axis)
        return [
            pltpu.SemaphoreType.DMA((size,)),
            pltpu.SemaphoreType.DMA((size,)),
            pltpu.SemaphoreType.DMA,
        ]

    def copy(self, away, block):
        other = (self.me + away) % self.size
        return pltpu.make_async_remote_copy(
            src_ref=self.src.at[other],
            dst_ref=self.dst.at[block],
            send_sem=self.send.at[away],
            recv_sem=self.recv.at[away],
            device_id={self.axis: other},
            device_id_type=MESH,
        )

    def start(self):
        for away in range(1, self.size):
            self.copy(away, self.me).start()
        pltpu.make_async_copy(self.src.at[self.me], self.dst.at[self.me], self.local).start()

    def finish(self):
        for away in range(1, self.size):
            self.copy(away, (self.me + self.size - away) % self.size).wait_recv()
        pltpu.make_async_copy(self.src.at[self.me], self.dst.at[self.me], self.local).wait()

    def drain(self):
        for away in range(1, self.size):
            self.copy(away, self.me).wait_send()


class Gather:
    def __init__(self, axis, src, at, send, recv, local, fast_first=False):
        self.axis, self.src, self.at = axis, src, at
        self.send, self.recv, self.local = send, recv, local
        n_slow, n_fast = plane(axis)
        self.me, slow, fast = place_in(axis)
        self.n, self.stride, self.pos = (n_slow, n_fast), (n_fast, 1), (slow, fast)
        if fast_first:
            self.n, self.stride, self.pos = (n_fast, n_slow), (1, n_fast), (fast, slow)

    @staticmethod
    def scratch(axis):
        size = lax.axis_size(axis)
        return [
            pltpu.SemaphoreType.DMA((4, size)),
            pltpu.SemaphoreType.DMA((size,)),
            pltpu.SemaphoreType.DMA,
        ]

    def copy(self, block, way, own=False):
        line, sign = way // 2, 1 - 2 * (way % 2)
        return pltpu.make_async_remote_copy(
            src_ref=self.src if own else self.at(block),
            dst_ref=self.at(block),
            send_sem=self.send.at[way, block],
            recv_sem=self.recv.at[block],
            device_id={self.axis: self.me + sign * self.stride[line]},
            device_id_type=MESH,
        )

    def open(self, way):
        line = way // 2
        return self.pos[line] < self.n[line] - 1 if way % 2 == 0 else self.pos[line] > 0

    def from_line(self, t):
        for way, sign in ((0, 1), (1, -1)):
            origin = self.pos[0] - sign * t
            there = (origin >= 0) & (origin < self.n[0])
            yield there, origin * self.stride[0] + self.pos[1] * self.stride[1], way

    def from_side(self, u):
        for z in range(self.n[0]):
            for way, sign in ((2, 1), (3, -1)):
                origin = self.pos[1] - sign * u
                there = (origin >= 0) & (origin < self.n[1])
                yield there, z * self.stride[0] + origin * self.stride[1], way

    def start(self):
        pltpu.make_async_copy(self.src, self.at(self.me), self.local).start()
        for way in range(4):

            @pl.when(self.open(way))
            def _():
                self.copy(self.me, way, True).start()

    def relay(self, t):
        for there, block, way in self.from_line(t):

            @pl.when(there)
            def _():
                self.copy(block, 0).wait_recv()
                for out in (way, 2, 3):

                    @pl.when(self.open(out))
                    def _():
                        self.copy(block, out).start()

    def steps(self):
        return self.n[0] - 1

    def finish(self):
        for u in range(1, self.n[1]):
            for there, block, way in self.from_side(u):

                @pl.when(there)
                def _():
                    self.copy(block, 0).wait_recv()
                    if self.n[1] > 2:

                        @pl.when(self.open(way))
                        def _():
                            self.copy(block, way).start()

    def drain(self):
        for way in range(4):

            @pl.when(self.open(way))
            def _():
                self.copy(self.me, way, True).wait_send()

        for t in range(1, self.n[0]):
            for there, block, way in self.from_line(t):
                for out in (way, 2, 3):

                    @pl.when(there & self.open(out))
                    def _():
                        self.copy(block, out).wait_send()

        if self.n[1] > 2:
            for u in range(1, self.n[1]):
                for there, block, way in self.from_side(u):

                    @pl.when(there & self.open(way))
                    def _():
                        self.copy(block, way).wait_send()

        pltpu.make_async_copy(self.src, self.at(self.me), self.local).wait()


def run_gathers(gathers):
    for g in gathers:
        g.start()
    for t in range(max(g.steps() for g in gathers)):
        for g in gathers:
            if t < g.steps():
                g.relay(t + 1)
    for g in gathers:
        g.finish()
    for g in gathers:
        g.drain()


def far_first(n, at):
    tables = []
    for a in range(n):
        tables.append(sorted(range(n), key=lambda t: (-abs(t - a), -t if a >= n / 2 else t)))
    places = []
    for k in range(n):
        value = jnp.int32(tables[0][k])
        for a in range(1, n):
            value = jnp.where(at == a, tables[a][k], value)
        places.append(value)
    return places


class Scatter:
    def __init__(self, axis, part, out, held, first, second, s_first, r_first, s_second, r_second, local):
        self.axis, self.part, self.out, self.held = axis, part, out, held
        self.first, self.second = first, second
        self.s_first, self.r_first, self.s_second, self.r_second = s_first, r_first, s_second, r_second
        self.local = local
        self.n_slow, self.n_fast = plane(axis)
        self.me, self.slow, self.fast = place_in(axis)
        self.order = far_first(self.n_slow, self.slow)
        self.fast_order = far_first(self.n_fast, self.fast)

    @staticmethod
    def scratch(axis, block, dtype):
        n_slow, n_fast = plane(axis)
        kept, ways = (1, 1) if n_fast == 2 else (n_fast, 2)
        return [
            pltpu.VMEM((n_slow, kept) + block, dtype),
            pltpu.VMEM((ways, n_fast - 1, n_slow) + block, dtype),
            pltpu.VMEM((2, n_slow - 1) + block, dtype),
            pltpu.SemaphoreType.DMA((2, n_fast, n_slow)),
            pltpu.SemaphoreType.DMA((2, n_fast, n_slow)),
            pltpu.SemaphoreType.DMA((2, n_slow)),
            pltpu.SemaphoreType.DMA((2, n_slow)),
            pltpu.SemaphoreType.DMA((n_slow, kept)),
        ]

    def mine(self, z):
        return self.held.at[z, 0 if self.n_fast == 2 else self.fast]

    def fast_slot(self, way, target, z):
        if self.n_fast == 2:
            return self.first.at[0, 0, z]
        return self.first.at[way, target - 1 if way == 0 else target, z]

    def fast_copy(self, way, target, z, own):
        slot = self.fast_slot(way, target, z)
        return pltpu.make_async_remote_copy(
            src_ref=self.part(z * self.n_fast + target) if own else slot,
            dst_ref=slot,
            send_sem=self.s_first.at[way, target, z],
            recv_sem=self.r_first.at[way, target, z],
            device_id={self.axis: self.me + (1 if way == 0 else -1)},
            device_id_type=MESH,
        )

    def slow_slot(self, way, target):
        return self.second.at[way, target - 1 if way == 0 else target]

    def slow_copy(self, way, target, own):
        slot = self.slow_slot(way, target)
        return pltpu.make_async_remote_copy(
            src_ref=self.mine(target) if own else slot,
            dst_ref=slot,
            send_sem=self.s_second.at[way, target],
            recv_sem=self.r_second.at[way, target],
            device_id={self.axis: self.me + (self.n_fast if way == 0 else -self.n_fast)},
            device_id_type=MESH,
        )

    def own_copies(self, z):
        targets = [self.fast] if self.n_fast == 2 else range(self.n_fast)
        return [
            pltpu.make_async_copy(
                self.part(z * self.n_fast + target), self.held.at[z, i], self.local.at[z, i]
            )
            for i, target in enumerate(targets)
        ]

    def edge(self, way):
        return self.fast == (0 if way == 0 else self.n_fast - 1)

    def slow_edge(self, way):
        return self.slow == (0 if way == 0 else self.n_slow - 1)

    def start(self):
        for z in self.order:
            for target in range(self.n_fast):
                for way in range(2):

                    @pl.when(self.edge(way) & (target > self.fast if way == 0 else target < self.fast))
                    def _():
                        self.fast_copy(way, target, z, True).start()

            for copy in self.own_copies(z):
                copy.start()

    def add(self, into, pieces, dtype):
        lead, rows = into.shape[:-2], into.shape[-2]
        tile = next((size for size in (64, 48, 32, 16) if rows % size == 0), rows)
        count = rows // tile

        def body(i, carry):
            if lead:
                at = (i // count, pl.ds(pl.multiple_of((i % count) * tile, tile), tile))
            else:
                at = (pl.ds(pl.multiple_of(i * tile, tile), tile),)
            if count == 1:
                at = (i,) if lead else ()
            at = at + (Ellipsis,)
            total = pieces[0][at].astype(F32)
            for piece in pieces[1:]:
                total = total + piece[at].astype(F32)
            into[at] = total.astype(dtype)
            return carry

        lax.fori_loop(0, count * (lead[0] if lead else 1), body, 0)

    def step(self, k):
        z = self.order[k]
        dtype = self.held.dtype
        for copy in self.own_copies(z):
            copy.wait()
        if self.n_fast > 2:
            for target in self.fast_order[:-1]:
                for way in range(2):
                    toward = target > self.fast if way == 0 else target < self.fast

                    @pl.when(jnp.logical_not(self.edge(way)) & toward)
                    def _():
                        self.fast_copy(way, target, z, False).wait_recv()
                        slot = self.fast_slot(way, target, z)
                        self.add(slot, [slot, self.held.at[z, target]], dtype)
                        self.fast_copy(way, target, z, False).start()

        held = self.mine(z)
        for way in range(2):

            @pl.when(jnp.logical_not(self.edge(way)))
            def _():
                self.fast_copy(way, self.fast, z, False).wait_recv()
                if self.n_fast > 2:
                    self.add(held, [held, self.fast_slot(way, self.fast, z)], dtype)

        extra = [self.first.at[0, 0, z]] if self.n_fast == 2 else []
        for way in range(2):
            toward = z > self.slow if way == 0 else z < self.slow

            @pl.when(toward & self.slow_edge(way))
            def _():
                if extra:
                    self.add(held, [held] + extra, dtype)
                self.slow_copy(way, z, True).start()

            @pl.when(toward & jnp.logical_not(self.slow_edge(way)))
            def _():
                self.slow_copy(way, z, False).wait_recv()
                slot = self.slow_slot(way, z)
                self.add(slot, [slot, held] + extra, dtype)
                self.slow_copy(way, z, False).start()

        if k == self.n_slow - 1:
            for way in range(2):

                @pl.when(jnp.logical_not(self.slow_edge(way)))
                def _():
                    self.slow_copy(way, self.slow, False).wait_recv()

            sums = [held] + extra
            lower, upper = self.slow_slot(0, self.slow), self.slow_slot(1, self.slow)
            odtype = self.out.dtype

            @pl.when(self.slow_edge(0))
            def _():
                self.add(self.out, sums + [upper], odtype)

            @pl.when(self.slow_edge(1))
            def _():
                self.add(self.out, sums + [lower], odtype)

            if self.n_slow > 2:

                @pl.when(jnp.logical_not(self.slow_edge(0) | self.slow_edge(1)))
                def _():
                    self.add(self.out, sums + [lower, upper], odtype)

    def steps(self):
        return self.n_slow

    def drain(self):
        for z in range(self.n_slow):
            for target in range(self.n_fast):
                for way in range(2):
                    toward = target > self.fast if way == 0 else target < self.fast

                    @pl.when(toward)
                    def _():
                        self.fast_copy(way, target, z, True).wait_send()

            for way in range(2):
                toward = z > self.slow if way == 0 else z < self.slow

                @pl.when(toward)
                def _():
                    self.slow_copy(way, z, True).wait_send()


class Spread:
    def __init__(self, axis, src, dst, send, recv, local):
        self.axis, self.src, self.dst = axis, src, dst
        self.send, self.recv, self.local = send, recv, local
        self.size = lax.axis_size(axis)
        self.me = lax.axis_index(axis)

    def copy(self, away, block):
        return pltpu.make_async_remote_copy(
            src_ref=self.src,
            dst_ref=self.dst.at[block],
            send_sem=self.send.at[away],
            recv_sem=self.recv.at[away],
            device_id={self.axis: (self.me + away) % self.size},
            device_id_type=MESH,
        )

    def start(self):
        for away in range(1, self.size):
            self.copy(away, self.me).start()
        pltpu.make_async_copy(self.src, self.dst.at[self.me], self.local).start()

    def finish(self):
        for away in range(1, self.size):
            self.copy(away, (self.me + self.size - away) % self.size).wait_recv()
        pltpu.make_async_copy(self.src, self.dst.at[self.me], self.local).wait()

    def drain(self):
        for away in range(1, self.size):
            self.copy(away, self.me).wait_send()


ANY = pl.BlockSpec(memory_space=pl.ANY)
IN_VMEM = pl.BlockSpec(memory_space=pltpu.VMEM)


def moving(kernel, number, operands, outs, out_specs, scratch, name, micros):
    return pl.pallas_call(
        kernel,
        out_shape=outs,
        in_specs=[ANY] * len(operands),
        out_specs=out_specs,
        scratch_shapes=scratch,
        cost_estimate=pl.CostEstimate(
            flops=0, bytes_accessed=int(micros * 3.6e6), transcendentals=0
        ),
        compiler_params=pltpu.CompilerParams(
            collective_id=number, has_side_effects=True, vmem_limit_bytes=56 * 2**20
        ),
        name=name,
    )(*operands)


def gather_blocks(axis, v, number, name, micros):
    def kernel(src, dst, *sems):
        greet([axis])
        run_gathers([Gather(axis, src, lambda block: dst.at[block], *sems)])

    shape = (lax.axis_size(axis),) + v.shape
    return moving(
        kernel, number, [v], jax.ShapeDtypeStruct(shape, v.dtype), ANY, Gather.scratch(axis), name, micros
    )


def scatter_blocks(axis, v, number, name, micros):
    def kernel(part, out, *scratch):
        greet([axis])
        work = Scatter(axis, lambda target: part.at[target], out, *scratch)
        work.start()
        for k in range(work.steps()):
            work.step(k)
        work.drain()

    block = v.shape[1:]
    return moving(
        kernel, number, [v], jax.ShapeDtypeStruct(block, F32), IN_VMEM,
        Scatter.scratch(axis, block, v.dtype), name, micros,
    )


def bring_weights(in_blocks, shared_blocks, out_rows, normed, up_rows, down_rows, shared_down, number):
    n_seq, n_dp = lax.axis_size("seq"), lax.axis_size("dp")
    operands = [in_blocks, shared_blocks, out_rows, normed, up_rows, down_rows, shared_down]
    seq_sems, dp_sems = Gather.scratch("seq"), Gather.scratch("dp")

    def kernel(
        in_blocks, shared_blocks, out_rows, normed, up_rows, down_rows, shared_down,
        in_mine, shared_mine, in_full, shared_full, out_full, normed_full, up_full, down_full,
        shared_down_full, *sems,
    ):
        sems = [sems[i : i + 3] for i in range(0, len(sems), 3)]
        greet(["seq", "dp"])
        swap_in = Exchange("seq", in_blocks, in_mine, *sems[0])
        swap_shared = Exchange("dp", shared_blocks, shared_mine, *sems[1])
        g_norm = Gather("seq", normed, lambda block: normed_full.at[block], *sems[2])
        g_up = Gather("seq", up_rows, lambda block: up_full.at[block], *sems[3])
        g_down = Gather("seq", down_rows, lambda block: down_full.at[:, block], *sems[4])
        g_sdown = Gather("seq", shared_down, lambda block: shared_down_full.at[block], *sems[5])
        g_shared = Gather("seq", shared_mine, lambda block: shared_full.at[block], *sems[6])
        g_in = Gather("dp", in_mine, lambda block: in_full.at[:, block], *sems[7])
        g_out = Gather("dp", out_rows, lambda block: out_full.at[block], *sems[8])
        swap_in.start()
        swap_shared.start()
        g_norm.start()
        swap_in.finish()
        g_in.start()
        g_out.start()
        swap_shared.finish()
        g_up.start()
        g_down.start()
        g_shared.start()
        g_sdown.start()
        lines = [g_norm, g_in, g_out, g_shared, g_sdown, g_up, g_down]
        for t in range(max(g.steps() for g in lines)):
            for g in lines:
                if t < g.steps():
                    g.relay(t + 1)
        for g in lines:
            g.finish()
        for g in lines + [swap_in, swap_shared]:
            g.drain()

    def like(shape):
        return jax.ShapeDtypeStruct(shape, BF)

    outs = [
        like(in_blocks.shape),
        like(shared_blocks.shape),
        like((n_seq, n_dp) + in_blocks.shape[1:]),
        like((n_seq,) + shared_blocks.shape),
        like((n_dp,) + out_rows.shape),
        like((n_seq,) + normed.shape),
        like((n_seq,) + up_rows.shape),
        like((down_rows.shape[0], n_seq) + down_rows.shape[1:]),
        like((n_seq,) + shared_down.shape),
    ]
    scratch = Exchange.scratch("seq") + Exchange.scratch("dp") + seq_sems * 5 + dp_sems * 2
    return moving(kernel, number, operands, outs, [ANY] * len(outs), scratch, "bring_weights", 90)[2:]


def return_grads(grad_in, grad_out, d_normed, grad_up, grad_down, grad_shared, grad_sdown, small, number):
    n_seq, n_dp = lax.axis_size("seq"), lax.axis_size("dp")
    operands = [grad_in, grad_out, d_normed, grad_up, grad_down, grad_shared, grad_sdown, small]
    blocks = [
        ("dp", (n_seq,) + grad_in.shape[2:], BF, BF),
        ("dp", grad_out.shape[1:], BF, F32),
        ("seq", d_normed.shape[1:], BF, F32),
        ("seq", grad_up.shape[1:], BF, F32),
        ("seq", (grad_down.shape[0],) + grad_down.shape[2:], BF, F32),
        ("seq", grad_shared.shape[1:], BF, BF),
        ("seq", grad_sdown.shape[1:], BF, F32),
    ]
    piece = small.shape[1:]

    def kernel(
        grad_in, grad_out, d_normed, grad_up, grad_down, grad_shared, grad_sdown, small,
        in_own, out_own, normed_own, up_own, down_own, shared_own, sdown_own, small_own,
        in_sum, shared_sum, piece_all, piece_dp, piece_seq, piece_sum, *rest,
    ):
        groups = [rest[8 * i : 8 * i + 8] for i in range(7)]
        sems = rest[56:]
        sems = [sems[i : i + 3] for i in range(0, len(sems), 3)]
        greet(["seq", "dp"])
        w_in = Scatter("dp", lambda b: grad_in.at[:, b], in_sum, *groups[0])
        w_out = Scatter("dp", lambda b: grad_out.at[b], out_own, *groups[1])
        normed = Scatter("seq", lambda b: d_normed.at[b], normed_own, *groups[2])
        up = Scatter("seq", lambda b: grad_up.at[b], up_own, *groups[3])
        down = Scatter("seq", lambda b: grad_down.at[:, b], down_own, *groups[4])
        shared = Scatter("seq", lambda b: grad_shared.at[b], shared_sum, *groups[5])
        sdown = Scatter("seq", lambda b: grad_sdown.at[b], sdown_own, *groups[6])
        swap_in = Exchange("seq", in_sum, in_own, *sems[0])
        swap_shared = Exchange("dp", shared_sum, shared_own, *sems[1])
        small_swap = Exchange("dp", small, piece_all, *sems[2])
        small_seq = Spread("seq", piece_dp, piece_seq, *sems[3])
        small_dp = Spread("dp", piece_sum, small_own, *sems[4])
        small_swap.start()
        for work in (w_in, normed, shared, w_out, up, down, sdown):
            work.start()
        across = [normed, shared, sdown, up, down]
        for work in across:
            work.step(0)
        small_swap.finish()
        piece_dp[...] = sum_leading(piece_all)
        small_seq.start()
        w_in.step(0)
        for k in range(1, normed.steps()):
            normed.step(k)
            shared.step(k)
            sdown.step(k)
        swap_shared.start()
        small_seq.finish()
        piece_sum[...] = sum_leading(piece_seq)
        small_dp.start()
        w_in.step(1)
        w_out.step(0)
        for k in range(1, up.steps()):
            up.step(k)
            down.step(k)
        for k in range(2, w_in.steps()):
            w_in.step(k)
        swap_in.start()
        for k in range(1, w_out.steps()):
            w_out.step(k)
        swap_shared.finish()
        small_dp.finish()
        swap_in.finish()
        for work in (w_in, w_out, normed, up, down, shared, sdown):
            work.drain()
        for work in (swap_in, swap_shared, small_swap, small_seq, small_dp):
            work.drain()

    outs = [
        jax.ShapeDtypeStruct(grad_in.shape[:1] + grad_in.shape[2:], BF),
        jax.ShapeDtypeStruct(blocks[1][1], F32),
        jax.ShapeDtypeStruct(blocks[2][1], F32),
        jax.ShapeDtypeStruct(blocks[3][1], F32),
        jax.ShapeDtypeStruct(blocks[4][1], F32),
        jax.ShapeDtypeStruct(blocks[5][1], BF),
        jax.ShapeDtypeStruct(blocks[6][1], F32),
        jax.ShapeDtypeStruct(small.shape, F32),
    ]
    scratch = [
        pltpu.VMEM(blocks[0][1], BF),
        pltpu.VMEM(blocks[5][1], BF),
        pltpu.VMEM((n_dp,) + piece, F32),
        pltpu.VMEM(piece, F32),
        pltpu.VMEM((n_seq,) + piece, F32),
        pltpu.VMEM(piece, F32),
    ]
    for axis, block, dtype, _ in blocks:
        scratch = scratch + Scatter.scratch(axis, block, dtype)
    scratch = scratch + Exchange.scratch("seq") + Exchange.scratch("dp") * 2
    scratch = scratch + Exchange.scratch("seq") + Exchange.scratch("dp")
    return moving(
        kernel, number, operands, outs, [IN_VMEM] * len(outs), scratch, "return_grads", 110
    )


def sum_leading(ref):
    total = ref[0]
    for i in range(1, ref.shape[0]):
        total = total + ref[i]
    return total


def pad_rows(pieces, rows=8):
    stacked = jnp.stack(pieces, 0)
    return jnp.pad(stacked, ((0, rows - stacked.shape[0]), (0, 0)))


def pad_lanes(v, width=LANES):
    return jnp.pad(v, ((0, 0),) * (v.ndim - 1) + ((0, width - v.shape[-1]),))


def matrix_rates():
    return (
        MATRIX_RATE * D ** (-0.5),
        MATRIX_RATE * (4 * D) ** (-0.5),
        MATRIX_RATE * D ** (-0.5),
        MATRIX_RATE * DI ** (-0.5),
        MATRIX_RATE * SF ** (-0.5),
        MATRIX_RATE * D ** (-0.5),
        MATRIX_RATE * (EF // TOPK) ** (-0.5),
    )


def adamw(weight, grad, first, second, rate, decay):
    first_new = BETA_ONE * first + (1.0 - BETA_ONE) * grad
    second_new = BETA_TWO * second + (1.0 - BETA_TWO) * grad * grad
    first_hat = first_new / (1.0 - BETA_ONE**STEP)
    second_hat = second_new / (1.0 - BETA_TWO**STEP)
    weight_new = weight - rate * (first_hat / (jnp.sqrt(second_hat) + ADAM_EPS) + decay * weight)
    return (weight_new, first_new, second_new)


def gather_rows(v, axis):
    return lax.all_gather(v, axis, axis=0, tiled=True)


def scatter_rows(v, axis):
    return lax.psum_scatter(v, axis, scatter_dimension=0, tiled=True)


def masked_gates(logits, mask):
    highest = jnp.max(jnp.where(mask > 0, logits, -jnp.inf), -1, keepdims=True)
    raised = jnp.where(mask > 0, jnp.exp(logits - highest), 0.0)
    return raised / jnp.sum(raised, -1, keepdims=True)


def on_device(
    tokens,
    seg_flags,
    routes,
    out_grad,
    w_in,
    w_in_m,
    w_in_v,
    w_router,
    w_router_m,
    w_router_v,
    w_shared_in,
    w_shared_in_m,
    w_shared_in_v,
    w_out,
    w_out_m,
    w_out_v,
    w_shared_out,
    w_shared_out_m,
    w_shared_out_v,
    w_experts_in,
    w_experts_in_m,
    w_experts_in_v,
    w_experts_out,
    w_experts_out_m,
    w_experts_out_v,
    small_params,
    small_m,
    small_v,
):
    n_seq = lax.axis_size("seq")
    n_dp = lax.axis_size("dp")
    at_seq = lax.axis_index("seq")
    at_dp = lax.axis_index("dp")
    experts = EXP_DEV * n_dp
    length = seg_flags.shape[1]
    hl = HEADS // n_seq
    cl = hl * HEAD_DIM
    cc = cl + 2 * STATE
    rows_in = w_in.shape[0]
    rows_out = w_out.shape[0]
    shared_rows = w_shared_out.shape[0]
    x_local = tokens[0].astype(F32)
    cotangent = out_grad[0].astype(F32)
    gain_one, conv_weight, conv_bias, dt_bias, a_log, d_skip, gain_mix, gain_two = unpack(
        small_params
    )

    low_in = w_in.astype(BF)
    gate_part = low_in[:, :DI].reshape(rows_in, n_seq, cl)
    conv_part = low_in[:, DI : 2 * DI].reshape(rows_in, n_seq, cl)
    both_part = low_in[:, 2 * DI : 2 * DI + 2 * STATE]
    step_part = low_in[:, DI + XBC :].reshape(rows_in, n_seq, hl)
    tail_part = pad_lanes(
        jnp.concatenate(
            [step_part, jnp.broadcast_to(w_router.astype(BF)[:, None, :], (rows_in, n_seq, experts))],
            2,
        )
    )
    width = 2 * cl + 2 * STATE + LANES
    in_blocks = jnp.concatenate(
        [
            gate_part,
            conv_part,
            jnp.broadcast_to(both_part[:, None, :], (rows_in, n_seq, 2 * STATE)),
            tail_part,
        ],
        2,
    ).transpose(1, 0, 2)
    mask = jnp.sum(
        (routes[0][:, :, None] == jnp.arange(experts)[None, None, :]).astype(F32), 1
    )
    cot_all = gather_rows(
        jnp.concatenate([out_grad[0], pad_lanes(mask.astype(BF))], 1), "dp"
    )
    mask_all = cot_all[:, D : D + experts].astype(F32)
    cot_all = cot_all[:, :D]

    sw = n_seq * shared_rows
    shared_blocks = (
        w_shared_in.astype(BF)
        .reshape(rows_in, 2, n_seq, n_dp, shared_rows)
        .transpose(3, 0, 1, 2, 4)
        .reshape(n_dp, rows_in, 2 * sw)
    )
    e_low = w_experts_in.astype(BF)
    up_rows = jnp.concatenate([e_low[0], e_low[1]], 1)
    root_one = lax.rsqrt(jnp.mean(x_local * x_local, -1, keepdims=True) + EPS)
    normed_low = (x_local * root_one * gain_one).astype(BF)
    in_full, shared_full, out_full, normed_all, up_full, down_full, shared_down = bring_weights(
        in_blocks,
        shared_blocks,
        w_out.astype(BF),
        normed_low,
        up_rows,
        w_experts_out.astype(BF),
        w_shared_out.astype(BF),
        1,
    )
    in_full = in_full.reshape(D, width)
    router = in_full[:, 2 * cl + 2 * STATE + hl : 2 * cl + 2 * STATE + hl + experts]
    out_full = out_full.reshape(cl, D)
    normed_all = normed_all.reshape(length, D)
    up_full = jnp.concatenate([up_full.reshape(D, 4 * EF), shared_full.reshape(D, 2 * sw)], 1)
    down_full = jnp.concatenate([down_full.reshape(2 * EF, D), shared_down.reshape(sw, D)], 0)
    ef_rows = w_experts_out.shape[1]

    projected = dot(normed_all, in_full)
    ids = jnp.cumsum(seg_flags[0])
    ids_behind = [
        jnp.concatenate([-jnp.ones((j,), ids.dtype), ids[: length - j]], 0) for j in range(KCONV)
    ]
    valid = [(behind == ids).astype(F32) for behind in ids_behind]
    cols = pad_lanes(jnp.stack(valid + [ids.astype(F32)], 1))
    rows = jnp.broadcast_to(
        ids.astype(F32).reshape(length // CHUNK, 1, CHUNK), (length // CHUNK, 8, CHUNK)
    )

    def local_channels(v):
        mine = lax.dynamic_slice_in_dim(v, at_seq * cl, cl, v.ndim - 1)
        return jnp.concatenate([mine, v[..., DI:]], -1)

    def local_heads(v):
        return lax.dynamic_slice_in_dim(v, at_seq * hl, hl)

    convp = jnp.pad(
        jnp.concatenate([local_channels(conv_weight), local_channels(conv_bias)[None]], 0),
        ((0, 8 - KCONV - 1), (0, 0)),
    )
    a_own = -jnp.exp(local_heads(a_log))
    headp = pad_rows([pad_lanes(local_heads(dt_bias)), pad_lanes(a_own)])
    chanp = pad_rows(
        [
            jnp.repeat(local_heads(d_skip), HEAD_DIM),
            lax.dynamic_slice_in_dim(gain_mix, at_seq * cl, cl),
        ]
    )
    gated_low, squares, mixer_out, states = mixer_forward(projected, cols, rows, convp, headp, chanp)
    mixed = scatter_blocks(
        "seq",
        jnp.concatenate(
            [dot(gated_low, out_full).astype(BF), pad_lanes(jnp.stack(split_two(squares[:, 0]), 1))],
            1,
        ).reshape(n_seq, length // n_seq, D + LANES),
        2,
        "sum_mixed",
        25,
    )
    square_sum = mixed[:, D : D + 1] + mixed[:, D + 1 : D + 2]
    mixed = mixed[:, :D]
    root_mix = lax.rsqrt(square_sum / DI + EPS)
    residual = x_local + root_mix * mixed
    root_two = lax.rsqrt(jnp.mean(residual * residual, -1, keepdims=True) + EPS)
    normed_two_low = (residual * root_two * gain_two).astype(BF)

    two_all = gather_blocks("dp", normed_two_low, 3, "gather_normed_two", 80).reshape(-1, D)
    gates_all = masked_gates(dot(two_all, router), mask_all)
    gates_own = lax.dynamic_slice_in_dim(gates_all, at_dp * EXP_DEV, EXP_DEV, 1)
    spread = jnp.concatenate(
        [
            jnp.broadcast_to(gates_own[:, 0:1], (gates_own.shape[0], EF)),
            jnp.broadcast_to(gates_own[:, 1:2], (gates_own.shape[0], EF)),
            jnp.ones((gates_own.shape[0], sw), F32),
        ],
        1,
    )
    joined = dot(two_all, up_full)
    gate_half = jnp.concatenate(
        [joined[:, :EF], joined[:, 2 * EF : 3 * EF], joined[:, 4 * EF : 4 * EF + sw]], 1
    )
    up_half = jnp.concatenate(
        [joined[:, EF : 2 * EF], joined[:, 3 * EF : 4 * EF], joined[:, 4 * EF + sw :]], 1
    )
    sig = jax.nn.sigmoid(gate_half)
    silu = gate_half * sig
    hidden = (silu * up_half).astype(BF).astype(F32)
    hidden_gated = (hidden * spread).astype(BF)
    moe = scatter_rows(dot(hidden_gated, down_full).astype(BF), "dp")
    block_out = (residual + moe.astype(F32)).astype(BF)

    d_hidden = dot_nt(cot_all, down_full)
    touched = hidden * d_hidden
    d_gate_zero = jnp.sum(touched[:, :EF], 1)
    d_gate_one = jnp.sum(touched[:, EF : 2 * EF], 1)
    d_hidden = d_hidden * spread
    d_gate_half = (d_hidden * up_half * (sig * (1.0 + gate_half * (1.0 - sig)))).astype(BF)
    d_up_half = (d_hidden * silu).astype(BF)
    d_joined = jnp.concatenate(
        [
            d_gate_half[:, :EF],
            d_up_half[:, :EF],
            d_gate_half[:, EF : 2 * EF],
            d_up_half[:, EF : 2 * EF],
            d_gate_half[:, 2 * EF :],
            d_up_half[:, 2 * EF :],
        ],
        1,
    )
    grad_up = dot_tn(two_all, d_joined[:, : 4 * EF]).astype(BF)
    grad_shared = dot_tn(two_all, d_joined[:, 4 * EF :]).astype(BF)
    grad_down = dot_tn(hidden_gated, cot_all).astype(BF)
    expert_place = jnp.arange(experts)[None, :]
    d_gates = jnp.where(expert_place == at_dp * EXP_DEV, d_gate_zero[:, None], 0.0) + jnp.where(
        expert_place == at_dp * EXP_DEV + 1, d_gate_one[:, None], 0.0
    )
    returned = scatter_blocks(
        "dp",
        jnp.concatenate(
            [dot_nt(d_joined, up_full).astype(BF), pad_lanes(jnp.concatenate(split_two(d_gates), 1))],
            1,
        ).reshape(n_dp, -1, D + LANES),
        4,
        "sum_d_normed_two",
        80,
    )
    d_gates = returned[:, D : D + experts] + returned[:, D + experts : D + 2 * experts]
    gates = masked_gates(dot(normed_two_low, router), mask)
    d_logits = gates * (d_gates - jnp.sum(gates * d_gates, 1, keepdims=True))
    d_logits = d_logits.astype(BF)
    grad_router = dot_tn(normed_two_low, d_logits)
    d_normed_two = returned[:, :D] + dot_nt(d_logits, router)
    grad_gain_two = jnp.sum(d_normed_two * residual * root_two, 0)
    scaled = d_normed_two * gain_two
    d_residual = (
        cotangent
        + scaled * root_two
        - residual * (root_two**3 / D * jnp.sum(scaled * residual, -1, keepdims=True))
    )
    residual_low = d_residual.astype(BF)
    along = jnp.sum(residual_low.astype(F32) * mixed, 1)
    packed = jnp.stack(split_two(root_mix[:, 0]) + split_two(along), 1)
    residual_all = gather_blocks(
        "seq", jnp.concatenate([residual_low, pad_lanes(packed)], 1), 5, "gather_residual", 25
    ).reshape(length, D + LANES)
    packed = residual_all[:, D : D + 4].astype(F32)
    residual_all = residual_all[:, :D]
    cols_back = jnp.concatenate(
        [cols[:, :5], packed[:, 0:1] + packed[:, 1:2], packed[:, 2:3] + packed[:, 3:4], cols[:, 7:]], 1
    )
    d_mixer = dot_nt(residual_all, out_full)
    d_proj, mixer_low, d_conv, d_head, d_chan = mixer_backward(
        projected, cols_back, rows, convp, headp, chanp, mixer_out, states, d_mixer
    )
    grad_out = dot_tn(mixer_low, residual_all)
    d_normed = dot_nt(d_proj, in_full).astype(BF)
    grad_in = dot_tn(normed_all, d_proj)
    grad_gain_one = jnp.sum(in_full.astype(F32) * grad_in, 1) / gain_one
    first_router = 2 * cl + 2 * STATE + hl
    grad_in = grad_in + jnp.pad(grad_router, ((0, 0), (first_router, width - first_router - experts)))

    def place_channels(v):
        base = jnp.zeros(v.shape[:-1] + (XBC,), F32)
        base = lax.dynamic_update_slice_in_dim(base, v[..., :cl], at_seq * cl, v.ndim - 1)
        return lax.dynamic_update_slice_in_dim(base, v[..., cl:], DI, v.ndim - 1)

    def place(v, whole):
        return lax.dynamic_update_slice_in_dim(
            jnp.zeros((whole,), F32), v, at_seq * v.shape[0], 0
        )

    small_local = jnp.concatenate(
        [
            grad_gain_one,
            place_channels(d_conv[:KCONV]).reshape(-1),
            place_channels(d_conv[KCONV]),
            place(d_head[0, :hl], HEADS),
            place(d_head[1, :hl], HEADS),
            place(jnp.sum(d_chan[0].reshape(hl, HEAD_DIM), 1), HEADS),
            place(d_chan[1], DI),
            grad_gain_two,
        ],
        0,
    )
    piece = -(-small_local.shape[0] // (n_dp * LANES * 8)) * 8
    small_blocks = jnp.pad(small_local, (0, n_dp * piece * LANES - small_local.shape[0]))
    (
        grad_in_own,
        grad_w_out,
        d_normed,
        grad_up_own,
        grad_w_experts_out,
        grad_shared_own,
        grad_w_shared_out,
        small_grad,
    ) = return_grads(
        grad_in.astype(BF).reshape(n_seq, n_dp, rows_in, width),
        grad_out.astype(BF).reshape(n_dp, rows_out, D),
        d_normed.reshape(n_seq, length // n_seq, D),
        grad_up.reshape(n_seq, D // n_seq, 4 * EF),
        grad_down[: 2 * EF].reshape(2, n_seq, ef_rows, D),
        grad_shared.reshape(n_seq, n_dp, rows_in, 2 * sw),
        grad_down[2 * EF :].reshape(n_seq, shared_rows, D),
        small_blocks.reshape(n_dp, piece, LANES),
        6,
    )
    grad_in_own = grad_in_own.astype(F32)
    grad_w_in = jnp.concatenate(
        [
            grad_in_own[:, :, :cl].transpose(1, 0, 2).reshape(rows_in, DI),
            grad_in_own[:, :, cl : 2 * cl].transpose(1, 0, 2).reshape(rows_in, DI),
            jnp.sum(grad_in_own[:, :, 2 * cl : 2 * cl + 2 * STATE], 0),
            grad_in_own[:, :, 2 * cl + 2 * STATE : first_router].transpose(1, 0, 2).reshape(rows_in, HEADS),
        ],
        1,
    )
    grad_w_router = jnp.sum(grad_in_own[:, :, first_router : first_router + experts], 0)
    grad_w_shared_in = (
        grad_shared_own.astype(F32)
        .reshape(n_dp, rows_in, 2, n_seq, shared_rows)
        .transpose(1, 2, 3, 0, 4)
        .reshape(rows_in, 2 * SF)
    )
    grad_w_experts_in = jnp.stack([grad_up_own[:, : 2 * EF], grad_up_own[:, 2 * EF :]], 0)
    small_grad = small_grad.reshape(-1)[: small_params.shape[0]]

    scaled = d_normed * gain_one
    input_grad = (
        d_residual
        + scaled * root_one
        - x_local * (root_one**3 / D * jnp.sum(scaled * x_local, -1, keepdims=True))
    )

    masters = (w_in, w_router, w_shared_in, w_out, w_shared_out, w_experts_in, w_experts_out)
    firsts = (
        w_in_m,
        w_router_m,
        w_shared_in_m,
        w_out_m,
        w_shared_out_m,
        w_experts_in_m,
        w_experts_out_m,
    )
    seconds = (
        w_in_v,
        w_router_v,
        w_shared_in_v,
        w_out_v,
        w_shared_out_v,
        w_experts_in_v,
        w_experts_out_v,
    )
    gradients = (
        grad_w_in,
        grad_w_router,
        grad_w_shared_in,
        grad_w_out,
        grad_w_shared_out,
        grad_w_experts_in,
        grad_w_experts_out,
    )
    rates = matrix_rates()
    results = [block_out[None], input_grad[None]]
    for member in range(7):
        results = results + list(
            adamw(
                masters[member],
                gradients[member],
                firsts[member],
                seconds[member],
                rates[member],
                DECAY_RATE,
            )
        )
    results = results + list(
        adamw(small_params, small_grad, small_m, small_v, SMALL_RATE, 0.0)
    )
    return tuple(results)


def solution(mesh):
    by_token = P("dp", "seq", None)
    dense = P(("seq", "dp"), None)
    expert = P("dp", "seq", None)
    weights = (dense,) * 15 + (expert,) * 6 + (P(),) * 3
    return jax.shard_map(
        on_device,
        mesh=mesh,
        in_specs=(by_token, P("dp", None), by_token, by_token) + weights,
        out_specs=(by_token, by_token) + weights,
        check_vma=False,
    )
```

```python
from functools import partial

import jax
import jax.numpy as jnp
from jax import lax
from jax.experimental import pallas as pl
from jax.experimental.pallas import tpu as pltpu
from jax.sharding import PartitionSpec as P

D = 1536
HEADS = 48
HEAD_DIM = 64
STATE = 128
KCONV = 4
EF = 512
SF = 1024
TOPK = 6
EXP_DEV = 2
STEP = 10
DI = 3072
XBC = 3328
LANES = 128
CHUNK = 256

EPS = 1e-05
BETA_ONE = 0.9
BETA_TWO = 0.95
ADAM_EPS = 1e-08
DECAY_RATE = 0.1
MATRIX_RATE = 0.4
SMALL_RATE = 0.2
HIGH = lax.Precision.HIGHEST
BF = jnp.bfloat16
F32 = jnp.float32
NT = (((1,), (1,)), ((), ()))
TN = (((0,), (0,)), ((), ()))


def unpack(small):
    widths = [D, KCONV * XBC, XBC, HEADS, HEADS, HEADS, DI, D]
    pieces = []
    offset = 0
    for extent in widths:
        pieces.append(small[offset : offset + extent])
        offset = offset + extent
    gain_one, conv_flat, conv_bias, dt_bias, a_log, d_skip, gain_mix, gain_two = pieces
    return (
        gain_one,
        conv_flat.reshape(KCONV, XBC),
        conv_bias,
        dt_bias,
        a_log,
        d_skip,
        gain_mix,
        gain_two,
    )


def dot(left, right):
    return jnp.dot(left, right, preferred_element_type=F32)


def dot_nt(left, right):
    return lax.dot_general(left, right, NT, preferred_element_type=F32)


def dot_tn(left, right):
    return lax.dot_general(left, right, TN, preferred_element_type=F32)


def softplus(v):
    return jnp.maximum(v, 0.0) + jnp.log1p(jnp.exp(-jnp.abs(v)))


def sigmoid(v):
    return 1.0 / (1.0 + jnp.exp(-v))


def split_two(v):
    upper = v.astype(BF)
    lower = (v - upper.astype(F32)).astype(BF)
    return upper, lower


def mixer_common(proj, halo, cols, rows, halo_cols, convp, headp, cl):
    q = proj.shape[0]
    cc = cl + 2 * STATE
    raw = proj[:, cl : cl + cc].astype(BF).astype(F32)
    before = halo[:, cl : cl + cc].astype(BF).astype(F32)
    padded = jnp.concatenate([before, raw], 0)
    pre = convp[KCONV : KCONV + 1, :] + jnp.zeros((q, cc), F32)
    taps = []
    for j in range(KCONV):
        tap = padded[8 - j : 8 - j + q] * cols[:, j : j + 1]
        taps.append(tap)
        pre = pre + convp[j : j + 1, :] * tap
    gate = sigmoid(pre)
    act = pre * gate
    b_low = act[:, cl : cl + STATE].astype(BF)
    c_low = act[:, cl + STATE :].astype(BF)
    dt = proj[:, cl + cc : cl + cc + LANES] + headp[0:1, :]
    step = softplus(dt)
    decay_log = step * headp[1:2, :]
    at_row = lax.broadcasted_iota(jnp.int32, (q, q), 0)
    at_col = lax.broadcasted_iota(jnp.int32, (q, q), 1)
    lower = (at_row >= at_col).astype(F32)
    cum = jnp.dot(lower, decay_log, preferred_element_type=F32, precision=HIGH)
    cum_t = cum.T
    id_col = cols[:, 4:5]
    id_row = rows[0:1, :]
    id_last = id_col[q - 1 : q, :]
    id_prev = halo_cols[7:8, 4:5]
    causal = (id_col == id_row) & (at_row >= at_col)
    cum_end = cum[q - 1 : q, :]
    entry = jnp.exp(cum) * (id_col == id_prev).astype(F32)
    tail = jnp.exp(cum_end - cum) * (id_col == id_last).astype(F32)
    carried = jnp.exp(cum_end) * (id_last == id_prev).astype(F32)
    scores = dot_nt(c_low, b_low)
    return dict(
        taps=taps, pre=pre, gate=gate, act=act, b=b_low, c=c_low, dt=dt, step=step,
        decay_log=decay_log, lower=lower, cum=cum, cum_t=cum_t, causal=causal,
        entry=entry, tail=tail, carried=carried, scores=scores,
    )


def pair_lanes(values, first, is_left):
    return jnp.where(is_left, values[:, first : first + 1], values[:, first + 1 : first + 2])


def head_decay(m, head):
    gaps = m["cum"][:, head : head + 1] - m["cum_t"][head : head + 1, :]
    return jnp.exp(jnp.where(m["causal"], gaps, -1e30))


def mixer_forward_kernel(
    cl, proj_ref, halo_ref, cols_ref, rows_ref, halo_cols_ref, convp_ref, headp_ref, chanp_ref,
    low_ref, square_ref, out_ref, states_ref, state,
):
    q = proj_ref.shape[0]
    pairs = cl // LANES

    @pl.when(pl.program_id(0) == 0)
    def _():
        state[...] = jnp.zeros_like(state)

    proj = proj_ref[...]
    m = mixer_common(
        proj, halo_ref[...], cols_ref[...], rows_ref[0], halo_cols_ref[...], convp_ref[...],
        headp_ref[...], cl,
    )
    is_left = lax.broadcasted_iota(jnp.int32, (q, LANES), 1) < HEAD_DIM
    top = lax.broadcasted_iota(jnp.int32, (LANES, LANES), 0) < HEAD_DIM
    square = jnp.zeros((q, 1), F32)
    for p in range(pairs):
        span = slice(p * LANES, (p + 1) * LANES)
        held = state[p]
        states_ref[0, p] = held
        inputs = m["act"][:, span]
        weighted = inputs * pair_lanes(m["step"], 2 * p, is_left)
        left = jnp.where(is_left, weighted, 0.0).astype(BF)
        right = jnp.where(is_left, 0.0, weighted).astype(BF)
        mix_left = (m["scores"] * head_decay(m, 2 * p)).astype(BF)
        mix_right = (m["scores"] * head_decay(m, 2 * p + 1)).astype(BF)
        out = dot(mix_left, left) + dot(mix_right, right)
        out = out + dot_nt(m["c"], held.astype(BF)) * pair_lanes(m["entry"], 2 * p, is_left)
        out = out + chanp_ref[0:1, span] * inputs
        tailed = (weighted * pair_lanes(m["tail"], 2 * p, is_left)).astype(BF)
        kept = jnp.where(top, m["carried"][:, 2 * p : 2 * p + 1], m["carried"][:, 2 * p + 1 : 2 * p + 2])
        state[p] = kept * held + dot_tn(tailed, m["b"])
        z = proj[:, span]
        gated = out * (z * sigmoid(z))
        out_ref[:, span] = out
        low_ref[:, span] = (gated * chanp_ref[1:2, span]).astype(BF)
        square = square + jnp.sum(gated * gated, 1, keepdims=True)
    square_ref[...] = jnp.broadcast_to(square, (q, LANES))


def mixer_backward_kernel(
    cl, proj_ref, halo_ref, cols_ref, rows_ref, halo_cols_ref, convp_ref, headp_ref, chanp_ref,
    out_ref, states_ref, dmix_ref,
    dproj_ref, mlow_ref, dconv_ref, dhead_ref, dchan_ref,
    dstate, ends, dpre_next,
):
    q = proj_ref.shape[0]
    pairs = cl // LANES
    cc = cl + 2 * STATE

    @pl.when(pl.program_id(0) == 0)
    def _():
        dstate[...] = jnp.zeros_like(dstate)
        ends[...] = jnp.zeros_like(ends)
        dpre_next[...] = jnp.zeros_like(dpre_next)
        dconv_ref[...] = jnp.zeros_like(dconv_ref)
        dhead_ref[...] = jnp.zeros_like(dhead_ref)
        dchan_ref[...] = jnp.zeros_like(dchan_ref)

    proj = proj_ref[...]
    cols = cols_ref[...]
    convp = convp_ref[...]
    headp = headp_ref[...]
    m = mixer_common(
        proj, halo_ref[...], cols, rows_ref[0], halo_cols_ref[...], convp, headp, cl
    )
    root = cols[:, 5:6]
    along = cols[:, 6:7] * (root * root * root) * (1.0 / DI)
    is_left = lax.broadcasted_iota(jnp.int32, (q, LANES), 1) < HEAD_DIM
    top = lax.broadcasted_iota(jnp.int32, (LANES, LANES), 0) < HEAD_DIM
    lane = lax.broadcasted_iota(jnp.int32, (1, LANES), 1)
    dscores = jnp.zeros((q, q), F32)
    d_c = jnp.zeros((q, STATE), F32)
    d_b = jnp.zeros((q, STATE), F32)
    gap_grad = jnp.zeros((q, LANES), F32)
    step_grad = jnp.zeros((q, LANES), F32)
    next_ends = jnp.zeros((1, LANES), F32)
    d_act = []
    for p in range(pairs):
        span = slice(p * LANES, (p + 1) * LANES)
        held = states_ref[0, p]
        held_low = held.astype(BF)
        after = dstate[p]
        after_low = after.astype(BF)
        inputs = m["act"][:, span]
        step_p = pair_lanes(m["step"], 2 * p, is_left)
        entry_p = pair_lanes(m["entry"], 2 * p, is_left)
        tail_p = pair_lanes(m["tail"], 2 * p, is_left)
        weighted = inputs * step_p
        w_low = weighted.astype(BF)
        z = proj[:, span]
        sig = sigmoid(z)
        silu = z * sig
        out = out_ref[:, span]
        gated = out * silu
        dmix = dmix_ref[:, span].astype(F32)
        gain = chanp_ref[1:2, span]
        mlow_ref[:, span] = (gated * gain * root).astype(BF)
        dchan_ref[1:2, span] += jnp.sum(gated * root * dmix, 0, keepdims=True)
        dgated = root * gain * dmix - gated * along
        d_out = dgated * silu
        dproj_ref[:, span] = (dgated * out * (sig * (1.0 + z * (1.0 - sig)))).astype(BF)
        dchan_ref[0:1, span] += jnp.sum(d_out * inputs, 0, keepdims=True)
        skip = chanp_ref[0:1, span]
        d_left = jnp.where(is_left, d_out, 0.0).astype(BF)
        d_right = jnp.where(is_left, 0.0, d_out).astype(BF)
        decay_left = head_decay(m, 2 * p)
        decay_right = head_decay(m, 2 * p + 1)
        mix_left = (m["scores"] * decay_left).astype(BF)
        mix_right = (m["scores"] * decay_right).astype(BF)
        d_within = dot_tn(mix_left, d_left) + dot_tn(mix_right, d_right)
        d_tailed = dot_nt(m["b"], after_low)
        d_weighted = d_within + tail_p * d_tailed
        tailed = (weighted * tail_p).astype(BF)
        dscores = dscores + dot_nt(d_left, w_low) * decay_left + dot_nt(d_right, w_low) * decay_right
        d_entered = (entry_p * d_out).astype(BF)
        d_c = d_c + dot(d_entered, held_low)
        d_b = d_b + dot(tailed, after_low)
        kept = jnp.where(top, m["carried"][:, 2 * p : 2 * p + 1], m["carried"][:, 2 * p + 1 : 2 * p + 2])
        before = kept * after + dot_tn(d_entered, m["c"])
        dstate[p] = before
        product = jnp.sum(before * held, 1, keepdims=True)
        end_left = jnp.sum(product[:HEAD_DIM], 0, keepdims=True)
        end_right = jnp.sum(product[HEAD_DIM:], 0, keepdims=True)
        next_ends = next_ends + jnp.where(lane == 2 * p, end_left, 0.0)
        next_ends = next_ends + jnp.where(lane == 2 * p + 1, end_right, 0.0)
        d_act.append(d_weighted * step_p + skip * d_out)
        through = (
            (d_left + d_right).astype(F32) * (out - skip * inputs)
            - w_low.astype(F32) * d_within
            - tailed.astype(F32) * d_tailed
        )
        for side in range(2):
            pick = is_left if side == 0 else jnp.logical_not(is_left)
            here = lane == 2 * p + side
            gap_grad = gap_grad + jnp.where(
                here, jnp.sum(jnp.where(pick, through, 0.0), 1, keepdims=True), 0.0
            )
            step_grad = step_grad + jnp.where(
                here, jnp.sum(jnp.where(pick, d_weighted * inputs, 0.0), 1, keepdims=True), 0.0
            )
    ds_low = dscores.astype(BF) if False else jnp.where(m["causal"], dscores, 0.0).astype(BF)
    d_c = d_c + dot(ds_low, m["b"])
    d_b = d_b + dot_tn(ds_low, m["c"])
    last = lax.broadcasted_iota(jnp.int32, (q, LANES), 0) == q - 1
    gap_grad = gap_grad + jnp.where(last, ends[0:1, :], 0.0)
    ends[0:1, :] = next_ends
    d_log = lax.dot_general(
        m["lower"], gap_grad, TN, preferred_element_type=F32, precision=HIGH
    )
    d_dt = (step_grad + d_log * headp[1:2, :]) * sigmoid(m["dt"])
    d_dt = jnp.where(lane < 2 * pairs, d_dt, 0.0)
    dhead_ref[0:1, :] += jnp.sum(d_dt, 0, keepdims=True)
    dhead_ref[1:2, :] += jnp.sum(d_log * m["decay_log"], 0, keepdims=True)
    dproj_ref[:, cl + cc : cl + cc + LANES] = d_dt.astype(BF)
    d_pre = jnp.concatenate(d_act + [d_b, d_c], 1)
    gate = m["gate"]
    d_pre = d_pre * (gate * (1.0 + m["pre"] * (1.0 - gate)))
    dconv_ref[KCONV : KCONV + 1, :] += jnp.sum(d_pre, 0, keepdims=True)
    d_raw = jnp.zeros((q, cc), F32)
    for j in range(KCONV):
        dconv_ref[j : j + 1, :] += jnp.sum(d_pre * m["taps"][j], 0, keepdims=True)
        spread = d_pre * (convp[j : j + 1, :] * cols[:, j : j + 1])
        if j == 0:
            d_raw = d_raw + spread
        else:
            joined = jnp.concatenate([spread, dpre_next[j]], 0)
            d_raw = d_raw + joined[j : j + q]
            dpre_next[j] = spread[:8]
    dproj_ref[:, cl : cl + cc] = d_raw.astype(BF)


def mixer_specs(width, cl, chunks, order):
    cc = cl + 2 * STATE
    halo = CHUNK // 8

    def before(i):
        return (jnp.maximum(order(i) * halo - 1, 0), 0)

    return [
        pl.BlockSpec((CHUNK, width), lambda i: (order(i), 0)),
        pl.BlockSpec((8, width), before),
        pl.BlockSpec((CHUNK, LANES), lambda i: (order(i), 0)),
        pl.BlockSpec((1, 8, CHUNK), lambda i: (order(i), 0, 0)),
        pl.BlockSpec((8, LANES), before),
        pl.BlockSpec((8, cc), lambda i: (0, 0)),
        pl.BlockSpec((8, LANES), lambda i: (0, 0)),
        pl.BlockSpec((8, cl), lambda i: (0, 0)),
    ]


def mixer_forward(projected, cols, rows, convp, headp, chanp):
    length, width = projected.shape
    cl = chanp.shape[1]
    chunks = length // CHUNK
    pairs = cl // LANES
    return pl.pallas_call(
        partial(mixer_forward_kernel, cl),
        grid=(chunks,),
        in_specs=mixer_specs(width, cl, chunks, lambda i: i),
        out_specs=[
            pl.BlockSpec((CHUNK, cl), lambda i: (i, 0)),
            pl.BlockSpec((CHUNK, LANES), lambda i: (i, 0)),
            pl.BlockSpec((CHUNK, cl), lambda i: (i, 0)),
            pl.BlockSpec((1, pairs, LANES, STATE), lambda i: (i, 0, 0, 0)),
        ],
        out_shape=[
            jax.ShapeDtypeStruct((length, cl), BF),
            jax.ShapeDtypeStruct((length, LANES), F32),
            jax.ShapeDtypeStruct((length, cl), F32),
            jax.ShapeDtypeStruct((chunks, pairs, LANES, STATE), F32),
        ],
        scratch_shapes=[pltpu.VMEM((pairs, LANES, STATE), F32)],
        compiler_params=pltpu.CompilerParams(vmem_limit_bytes=56 * 2**20),
        name="mixer_forward",
    )(projected, projected, cols, rows, cols, convp, headp, chanp)


def mixer_backward(projected, cols, rows, convp, headp, chanp, out, states, dmix):
    length, width = projected.shape
    cl = chanp.shape[1]
    cc = cl + 2 * STATE
    chunks = length // CHUNK
    pairs = cl // LANES

    def order(i):
        return chunks - 1 - i

    return pl.pallas_call(
        partial(mixer_backward_kernel, cl),
        grid=(chunks,),
        in_specs=mixer_specs(width, cl, chunks, order)
        + [
            pl.BlockSpec((CHUNK, cl), lambda i: (order(i), 0)),
            pl.BlockSpec((1, pairs, LANES, STATE), lambda i: (order(i), 0, 0, 0)),
            pl.BlockSpec((CHUNK, cl), lambda i: (order(i), 0)),
        ],
        out_specs=[
            pl.BlockSpec((CHUNK, width), lambda i: (order(i), 0)),
            pl.BlockSpec((CHUNK, cl), lambda i: (order(i), 0)),
            pl.BlockSpec((8, cc), lambda i: (0, 0)),
            pl.BlockSpec((8, LANES), lambda i: (0, 0)),
            pl.BlockSpec((8, cl), lambda i: (0, 0)),
        ],
        out_shape=[
            jax.ShapeDtypeStruct((length, width), BF),
            jax.ShapeDtypeStruct((length, cl), BF),
            jax.ShapeDtypeStruct((8, cc), F32),
            jax.ShapeDtypeStruct((8, LANES), F32),
            jax.ShapeDtypeStruct((8, cl), F32),
        ],
        scratch_shapes=[
            pltpu.VMEM((pairs, LANES, STATE), F32),
            pltpu.VMEM((8, LANES), F32),
            pltpu.VMEM((KCONV, 8, cc), F32),
        ],
        compiler_params=pltpu.CompilerParams(vmem_limit_bytes=56 * 2**20),
        name="mixer_backward",
    )(projected, projected, cols, rows, cols, convp, headp, chanp, out, states, dmix)


MESH = pl.DeviceIdType.MESH


def plane(axis):
    size = lax.axis_size(axis)
    fast = 2 if axis == "seq" else max(1, size // 4)
    return size // fast, fast


def place_in(axis):
    n_slow, n_fast = plane(axis)
    me = lax.axis_index(axis)
    return me, me // n_fast, me % n_fast


def greet(axes):
    barrier = pltpu.get_barrier_semaphore()
    count = 0
    for axis in axes:
        size = lax.axis_size(axis)
        me = lax.axis_index(axis)
        for away in range(1, size):
            pl.semaphore_signal(
                barrier, inc=1, device_id={axis: (me + away) % size}, device_id_type=MESH
            )
        count = count + size - 1
    pl.semaphore_wait(barrier, count)


class Exchange:
    def __init__(self, axis, src, dst, send, recv, local):
        self.axis, self.src, self.dst = axis, src, dst
        self.send, self.recv, self.local = send, recv, local
        self.size = lax.axis_size(axis)
        self.me = lax.axis_index(axis)

    @staticmethod
    def scratch(axis):
        size = lax.axis_size(axis)
        return [
            pltpu.SemaphoreType.DMA((size,)),
            pltpu.SemaphoreType.DMA((size,)),
            pltpu.SemaphoreType.DMA,
        ]

    def copy(self, away, block):
        other = (self.me + away) % self.size
        return pltpu.make_async_remote_copy(
            src_ref=self.src.at[other],
            dst_ref=self.dst.at[block],
            send_sem=self.send.at[away],
            recv_sem=self.recv.at[away],
            device_id={self.axis: other},
            device_id_type=MESH,
        )

    def start(self):
        for away in range(1, self.size):
            self.copy(away, self.me).start()
        pltpu.make_async_copy(self.src.at[self.me], self.dst.at[self.me], self.local).start()

    def finish(self):
        for away in range(1, self.size):
            self.copy(away, (self.me + self.size - away) % self.size).wait_recv()
        pltpu.make_async_copy(self.src.at[self.me], self.dst.at[self.me], self.local).wait()

    def drain(self):
        for away in range(1, self.size):
            self.copy(away, self.me).wait_send()


class Gather:
    def __init__(self, axis, src, at, send, recv, local, fast_first=False):
        self.axis, self.src, self.at = axis, src, at
        self.send, self.recv, self.local = send, recv, local
        n_slow, n_fast = plane(axis)
        self.me, slow, fast = place_in(axis)
        self.n, self.stride, self.pos = (n_slow, n_fast), (n_fast, 1), (slow, fast)
        if fast_first:
            self.n, self.stride, self.pos = (n_fast, n_slow), (1, n_fast), (fast, slow)

    @staticmethod
    def scratch(axis):
        size = lax.axis_size(axis)
        return [
            pltpu.SemaphoreType.DMA((4, size)),
            pltpu.SemaphoreType.DMA((size,)),
            pltpu.SemaphoreType.DMA,
        ]

    def copy(self, block, way, own=False):
        line, sign = way // 2, 1 - 2 * (way % 2)
        return pltpu.make_async_remote_copy(
            src_ref=self.src if own else self.at(block),
            dst_ref=self.at(block),
            send_sem=self.send.at[way, block],
            recv_sem=self.recv.at[block],
            device_id={self.axis: self.me + sign * self.stride[line]},
            device_id_type=MESH,
        )

    def open(self, way):
        line = way // 2
        return self.pos[line] < self.n[line] - 1 if way % 2 == 0 else self.pos[line] > 0

    def from_line(self, t):
        for way, sign in ((0, 1), (1, -1)):
            origin = self.pos[0] - sign * t
            there = (origin >= 0) & (origin < self.n[0])
            yield there, origin * self.stride[0] + self.pos[1] * self.stride[1], way

    def from_side(self, u):
        for z in range(self.n[0]):
            for way, sign in ((2, 1), (3, -1)):
                origin = self.pos[1] - sign * u
                there = (origin >= 0) & (origin < self.n[1])
                yield there, z * self.stride[0] + origin * self.stride[1], way

    def start(self):
        pltpu.make_async_copy(self.src, self.at(self.me), self.local).start()
        for way in range(4):

            @pl.when(self.open(way))
            def _():
                self.copy(self.me, way, True).start()

    def relay(self, t):
        for there, block, way in self.from_line(t):

            @pl.when(there)
            def _():
                self.copy(block, 0).wait_recv()
                for out in (way, 2, 3):

                    @pl.when(self.open(out))
                    def _():
                        self.copy(block, out).start()

    def steps(self):
        return self.n[0] - 1

    def finish(self):
        for u in range(1, self.n[1]):
            for there, block, way in self.from_side(u):

                @pl.when(there)
                def _():
                    self.copy(block, 0).wait_recv()
                    if self.n[1] > 2:

                        @pl.when(self.open(way))
                        def _():
                            self.copy(block, way).start()

    def settle(self):
        pltpu.make_async_copy(self.src, self.at(self.me), self.local).wait()

    def drain(self, settle=True):
        for way in range(4):

            @pl.when(self.open(way))
            def _():
                self.copy(self.me, way, True).wait_send()

        for t in range(1, self.n[0]):
            for there, block, way in self.from_line(t):
                for out in (way, 2, 3):

                    @pl.when(there & self.open(out))
                    def _():
                        self.copy(block, out).wait_send()

        if self.n[1] > 2:
            for u in range(1, self.n[1]):
                for there, block, way in self.from_side(u):

                    @pl.when(there & self.open(way))
                    def _():
                        self.copy(block, way).wait_send()

        if settle:
            self.settle()


def run_gathers(gathers):
    for g in gathers:
        g.start()
    for t in range(max(g.steps() for g in gathers)):
        for g in gathers:
            if t < g.steps():
                g.relay(t + 1)
    for g in gathers:
        g.finish()
    for g in gathers:
        g.drain()


def far_first(n, at):
    tables = []
    for a in range(n):
        tables.append(sorted(range(n), key=lambda t: (-abs(t - a), -t if a >= n / 2 else t)))
    places = []
    for k in range(n):
        value = jnp.int32(tables[0][k])
        for a in range(1, n):
            value = jnp.where(at == a, tables[a][k], value)
        places.append(value)
    return places


class Scatter:
    def __init__(self, axis, part, out, held, first, second, s_first, r_first, s_second, r_second, local):
        self.axis, self.part, self.out, self.held = axis, part, out, held
        self.first, self.second = first, second
        self.s_first, self.r_first, self.s_second, self.r_second = s_first, r_first, s_second, r_second
        self.local = local
        self.n_slow, self.n_fast = plane(axis)
        self.me, self.slow, self.fast = place_in(axis)
        self.order = far_first(self.n_slow, self.slow)
        self.fast_order = far_first(self.n_fast, self.fast)

    @staticmethod
    def scratch(axis, block, dtype):
        n_slow, n_fast = plane(axis)
        kept, ways = (1, 1) if n_fast == 2 else (n_fast, 2)
        return [
            pltpu.VMEM((n_slow, kept) + block, dtype),
            pltpu.VMEM((ways, n_fast - 1, n_slow) + block, dtype),
            pltpu.VMEM((2, n_slow - 1) + block, dtype),
            pltpu.SemaphoreType.DMA((2, n_fast, n_slow)),
            pltpu.SemaphoreType.DMA((2, n_fast, n_slow)),
            pltpu.SemaphoreType.DMA((2, n_slow)),
            pltpu.SemaphoreType.DMA((2, n_slow)),
            pltpu.SemaphoreType.DMA((n_slow, kept)),
        ]

    def mine(self, z):
        return self.held.at[z, 0 if self.n_fast == 2 else self.fast]

    def fast_slot(self, way, target, z):
        if self.n_fast == 2:
            return self.first.at[0, 0, z]
        return self.first.at[way, target - 1 if way == 0 else target, z]

    def fast_copy(self, way, target, z, own):
        slot = self.fast_slot(way, target, z)
        return pltpu.make_async_remote_copy(
            src_ref=self.part(z * self.n_fast + target) if own else slot,
            dst_ref=slot,
            send_sem=self.s_first.at[way, target, z],
            recv_sem=self.r_first.at[way, target, z],
            device_id={self.axis: self.me + (1 if way == 0 else -1)},
            device_id_type=MESH,
        )

    def slow_slot(self, way, target):
        return self.second.at[way, target - 1 if way == 0 else target]

    def slow_copy(self, way, target, own):
        slot = self.slow_slot(way, target)
        return pltpu.make_async_remote_copy(
            src_ref=self.mine(target) if own else slot,
            dst_ref=slot,
            send_sem=self.s_second.at[way, target],
            recv_sem=self.r_second.at[way, target],
            device_id={self.axis: self.me + (self.n_fast if way == 0 else -self.n_fast)},
            device_id_type=MESH,
        )

    def own_copies(self, z):
        targets = [self.fast] if self.n_fast == 2 else range(self.n_fast)
        return [
            pltpu.make_async_copy(
                self.part(z * self.n_fast + target), self.held.at[z, i], self.local.at[z, i]
            )
            for i, target in enumerate(targets)
        ]

    def edge(self, way):
        return self.fast == (0 if way == 0 else self.n_fast - 1)

    def slow_edge(self, way):
        return self.slow == (0 if way == 0 else self.n_slow - 1)

    def start(self):
        for z in self.order:
            for target in range(self.n_fast):
                for way in range(2):

                    @pl.when(self.edge(way) & (target > self.fast if way == 0 else target < self.fast))
                    def _():
                        self.fast_copy(way, target, z, True).start()

            for copy in self.own_copies(z):
                copy.start()

    def add(self, into, pieces, dtype):
        lead, rows = into.shape[:-2], into.shape[-2]
        tile = 16 if rows % 16 == 0 else rows
        count = rows // tile

        def body(i, carry):
            if lead:
                at = (i // count, pl.ds(pl.multiple_of((i % count) * tile, tile), tile))
            else:
                at = (pl.ds(pl.multiple_of(i * tile, tile), tile),)
            if count == 1:
                at = (i,) if lead else ()
            at = at + (Ellipsis,)
            total = pieces[0][at].astype(F32)
            for piece in pieces[1:]:
                total = total + piece[at].astype(F32)
            into[at] = total.astype(dtype)
            return carry

        lax.fori_loop(0, count * (lead[0] if lead else 1), body, 0)

    def step(self, k):
        z = self.order[k]
        dtype = self.held.dtype
        for copy in self.own_copies(z):
            copy.wait()
        if self.n_fast > 2:
            for target in self.fast_order[:-1]:
                for way in range(2):
                    toward = target > self.fast if way == 0 else target < self.fast

                    @pl.when(jnp.logical_not(self.edge(way)) & toward)
                    def _():
                        self.fast_copy(way, target, z, False).wait_recv()
                        slot = self.fast_slot(way, target, z)
                        self.add(slot, [slot, self.held.at[z, target]], dtype)
                        self.fast_copy(way, target, z, False).start()

        held = self.mine(z)
        for way in range(2):

            @pl.when(jnp.logical_not(self.edge(way)))
            def _():
                self.fast_copy(way, self.fast, z, False).wait_recv()
                if self.n_fast > 2:
                    self.add(held, [held, self.fast_slot(way, self.fast, z)], dtype)

        extra = [self.first.at[0, 0, z]] if self.n_fast == 2 else []
        for way in range(2):
            toward = z > self.slow if way == 0 else z < self.slow

            @pl.when(toward & self.slow_edge(way))
            def _():
                if extra:
                    self.add(held, [held] + extra, dtype)
                self.slow_copy(way, z, True).start()

            @pl.when(toward & jnp.logical_not(self.slow_edge(way)))
            def _():
                self.slow_copy(way, z, False).wait_recv()
                slot = self.slow_slot(way, z)
                self.add(slot, [slot, held] + extra, dtype)
                self.slow_copy(way, z, False).start()

        if k == self.n_slow - 1:
            for way in range(2):

                @pl.when(jnp.logical_not(self.slow_edge(way)))
                def _():
                    self.slow_copy(way, self.slow, False).wait_recv()

            sums = [held] + extra
            lower, upper = self.slow_slot(0, self.slow), self.slow_slot(1, self.slow)
            odtype = self.out.dtype

            @pl.when(self.slow_edge(0))
            def _():
                self.add(self.out, sums + [upper], odtype)

            @pl.when(self.slow_edge(1))
            def _():
                self.add(self.out, sums + [lower], odtype)

            if self.n_slow > 2:

                @pl.when(jnp.logical_not(self.slow_edge(0) | self.slow_edge(1)))
                def _():
                    self.add(self.out, sums + [lower, upper], odtype)

    def steps(self):
        return self.n_slow

    def drain(self):
        for z in range(self.n_slow):
            for target in range(self.n_fast):
                for way in range(2):
                    toward = target > self.fast if way == 0 else target < self.fast

                    @pl.when(toward)
                    def _():
                        self.fast_copy(way, target, z, True).wait_send()

            for way in range(2):
                toward = z > self.slow if way == 0 else z < self.slow

                @pl.when(toward)
                def _():
                    self.slow_copy(way, z, True).wait_send()


class Spread:
    def __init__(self, axis, src, dst, send, recv, local):
        self.axis, self.src, self.dst = axis, src, dst
        self.send, self.recv, self.local = send, recv, local
        self.size = lax.axis_size(axis)
        self.me = lax.axis_index(axis)

    def copy(self, away, block):
        return pltpu.make_async_remote_copy(
            src_ref=self.src,
            dst_ref=self.dst.at[block],
            send_sem=self.send.at[away],
            recv_sem=self.recv.at[away],
            device_id={self.axis: (self.me + away) % self.size},
            device_id_type=MESH,
        )

    def start(self):
        for away in range(1, self.size):
            self.copy(away, self.me).start()
        pltpu.make_async_copy(self.src, self.dst.at[self.me], self.local).start()

    def finish(self):
        for away in range(1, self.size):
            self.copy(away, (self.me + self.size - away) % self.size).wait_recv()
        pltpu.make_async_copy(self.src, self.dst.at[self.me], self.local).wait()

    def drain(self):
        for away in range(1, self.size):
            self.copy(away, self.me).wait_send()


ANY = pl.BlockSpec(memory_space=pl.ANY)
IN_VMEM = pl.BlockSpec(memory_space=pltpu.VMEM)


def moving(kernel, number, operands, outs, out_specs, scratch, name, micros, source=ANY):
    return pl.pallas_call(
        kernel,
        out_shape=outs,
        in_specs=[source] * len(operands),
        out_specs=out_specs,
        scratch_shapes=scratch,
        cost_estimate=pl.CostEstimate(
            flops=0, bytes_accessed=int(micros * 3.6e6), transcendentals=0
        ),
        compiler_params=pltpu.CompilerParams(
            collective_id=number, has_side_effects=True, vmem_limit_bytes=56 * 2**20
        ),
        name=name,
    )(*operands)


def gather_blocks(axis, v, number, name, micros):
    def kernel(src, dst, *sems):
        greet([axis])
        run_gathers([Gather(axis, src, lambda block: dst.at[block], *sems)])

    shape = (lax.axis_size(axis),) + v.shape
    return moving(
        kernel, number, [v], jax.ShapeDtypeStruct(shape, v.dtype), ANY, Gather.scratch(axis), name,
        micros, IN_VMEM,
    )


def scatter_blocks(axis, v, number, name, micros):
    def kernel(part, out, *scratch):
        greet([axis])
        work = Scatter(axis, lambda target: part.at[target], out, *scratch)
        work.start()
        for k in range(work.steps()):
            work.step(k)
        work.drain()

    block = v.shape[1:]
    return moving(
        kernel, number, [v], jax.ShapeDtypeStruct(block, F32), IN_VMEM,
        Scatter.scratch(axis, block, v.dtype), name, micros,
    )


def bring_weights(in_blocks, shared_blocks, out_rows, normed, up_rows, down_rows, shared_down, number):
    n_seq, n_dp = lax.axis_size("seq"), lax.axis_size("dp")
    operands = [in_blocks, shared_blocks, out_rows, normed, up_rows, down_rows, shared_down]
    seq_sems, dp_sems = Gather.scratch("seq"), Gather.scratch("dp")

    def kernel(
        in_blocks, shared_blocks, out_rows, normed, up_rows, down_rows, shared_down,
        in_full, shared_full, out_full, normed_full, up_full, down_full, shared_down_full,
        in_mine, shared_mine, *sems,
    ):
        sems = [sems[i : i + 3] for i in range(0, len(sems), 3)]
        greet(["seq", "dp"])
        swap_in = Exchange("seq", in_blocks, in_mine, *sems[0])
        swap_shared = Exchange("dp", shared_blocks, shared_mine, *sems[1])
        g_norm = Gather("seq", normed, lambda block: normed_full.at[block], *sems[2])
        g_up = Gather("seq", up_rows, lambda block: up_full.at[block], *sems[3])
        g_down = Gather("seq", down_rows, lambda block: down_full.at[:, block], *sems[4])
        g_sdown = Gather("seq", shared_down, lambda block: shared_down_full.at[block], *sems[5])
        g_shared = Gather("seq", shared_mine, lambda block: shared_full.at[block], *sems[6])
        g_in = Gather("dp", in_mine, lambda block: in_full.at[:, block], *sems[7])
        g_out = Gather("dp", out_rows, lambda block: out_full.at[block], *sems[8])
        swap_in.start()
        swap_shared.start()
        swap_in.finish()
        g_in.start()
        g_norm.start()
        g_out.start()
        g_up.start()
        g_down.start()
        swap_shared.finish()
        g_shared.start()
        g_sdown.start()
        rows = [g_in, g_out]
        lines = [g_norm, g_up, g_down, g_shared, g_sdown]
        for t in range(1, g_in.steps() + 1):
            for g in rows:
                g.relay(t)
            if t == 1:
                g_norm.relay(1)
        for t in range(1, g_norm.steps() + 1):
            for g in lines:
                if g is not g_norm or t > 1:
                    g.relay(t)
        lines = rows + lines
        for g in lines:
            g.finish()
        for g in lines + [swap_in, swap_shared]:
            g.drain()

    def like(shape):
        return jax.ShapeDtypeStruct(shape, BF)

    outs = [
        like((n_seq, n_dp) + in_blocks.shape[1:]),
        like((n_seq,) + shared_blocks.shape),
        like((n_dp,) + out_rows.shape),
        like((n_seq,) + normed.shape),
        like((n_seq,) + up_rows.shape),
        like((down_rows.shape[0], n_seq) + down_rows.shape[1:]),
        like((n_seq,) + shared_down.shape),
    ]
    scratch = [pltpu.VMEM(in_blocks.shape, BF), pltpu.VMEM(shared_blocks.shape, BF)]
    scratch = scratch + Exchange.scratch("seq") + Exchange.scratch("dp") + seq_sems * 5 + dp_sems * 2
    return moving(
        kernel, number, operands, outs, [ANY] * len(outs), scratch, "bring_weights", 100, IN_VMEM
    )


def return_grads(grad_in, grad_out, d_normed, grad_up, grad_down, grad_shared, grad_sdown, small, number):
    n_seq, n_dp = lax.axis_size("seq"), lax.axis_size("dp")
    operands = [grad_in, grad_out, d_normed, grad_up, grad_down, grad_shared, grad_sdown, small]
    blocks = [
        ("dp", (n_seq,) + grad_in.shape[2:], BF, BF),
        ("dp", grad_out.shape[1:], BF, F32),
        ("seq", d_normed.shape[1:], BF, F32),
        ("seq", grad_up.shape[1:], BF, F32),
        ("seq", (grad_down.shape[0],) + grad_down.shape[2:], BF, F32),
        ("seq", grad_shared.shape[1:], BF, BF),
        ("seq", grad_sdown.shape[1:], BF, F32),
    ]
    piece = small.shape[1:]

    def kernel(
        grad_in, grad_out, d_normed, grad_up, grad_down, grad_shared, grad_sdown, small,
        in_own, out_own, normed_own, up_own, down_own, shared_own, sdown_own, small_own,
        in_sum, shared_sum, piece_all, piece_dp, piece_seq, piece_sum, *rest,
    ):
        groups = [rest[8 * i : 8 * i + 8] for i in range(7)]
        sems = rest[56:]
        sems = [sems[i : i + 3] for i in range(0, len(sems), 3)]
        greet(["seq", "dp"])
        w_in = Scatter("dp", lambda b: grad_in.at[:, b], in_sum, *groups[0])
        w_out = Scatter("dp", lambda b: grad_out.at[b], out_own, *groups[1])
        normed = Scatter("seq", lambda b: d_normed.at[b], normed_own, *groups[2])
        up = Scatter("seq", lambda b: grad_up.at[b], up_own, *groups[3])
        down = Scatter("seq", lambda b: grad_down.at[:, b], down_own, *groups[4])
        shared = Scatter("seq", lambda b: grad_shared.at[b], shared_sum, *groups[5])
        sdown = Scatter("seq", lambda b: grad_sdown.at[b], sdown_own, *groups[6])
        swap_in = Exchange("seq", in_sum, in_own, *sems[0])
        swap_shared = Exchange("dp", shared_sum, shared_own, *sems[1])
        small_swap = Exchange("dp", small, piece_all, *sems[2])
        small_seq = Spread("seq", piece_dp, piece_seq, *sems[3])
        small_dp = Spread("dp", piece_sum, small_own, *sems[4])
        small_swap.start()
        for work in (w_in, normed, shared, sdown, w_out, up, down):
            work.start()
        across = [normed, shared, sdown, up, down]
        for work in across:
            work.step(0)
        w_in.step(0)
        w_in.step(1)
        small_swap.finish()
        piece_dp[...] = sum_leading(piece_all)
        small_seq.start()
        for k in range(1, normed.steps()):
            normed.step(k)
            shared.step(k)
            sdown.step(k)
        swap_shared.start()
        for k in range(2, w_in.steps()):
            w_in.step(k)
        swap_in.start()
        w_out.step(0)
        for k in range(1, up.steps()):
            down.step(k)
            up.step(k)
        small_seq.finish()
        piece_sum[...] = sum_leading(piece_seq)
        small_dp.start()
        for k in range(1, w_out.steps()):
            w_out.step(k)
        swap_shared.finish()
        small_dp.finish()
        swap_in.finish()
        for work in (w_in, w_out, normed, up, down, shared, sdown):
            work.drain()
        for work in (swap_in, swap_shared, small_swap, small_seq, small_dp):
            work.drain()

    outs = [
        jax.ShapeDtypeStruct(grad_in.shape[:1] + grad_in.shape[2:], BF),
        jax.ShapeDtypeStruct(blocks[1][1], F32),
        jax.ShapeDtypeStruct(blocks[2][1], F32),
        jax.ShapeDtypeStruct(blocks[3][1], F32),
        jax.ShapeDtypeStruct(blocks[4][1], F32),
        jax.ShapeDtypeStruct(blocks[5][1], BF),
        jax.ShapeDtypeStruct(blocks[6][1], F32),
        jax.ShapeDtypeStruct(small.shape, F32),
    ]
    scratch = [
        pltpu.VMEM(blocks[0][1], BF),
        pltpu.VMEM(blocks[5][1], BF),
        pltpu.VMEM((n_dp,) + piece, F32),
        pltpu.VMEM(piece, F32),
        pltpu.VMEM((n_seq,) + piece, F32),
        pltpu.VMEM(piece, F32),
    ]
    for axis, block, dtype, _ in blocks:
        scratch = scratch + Scatter.scratch(axis, block, dtype)
    scratch = scratch + Exchange.scratch("seq") + Exchange.scratch("dp") * 2
    scratch = scratch + Exchange.scratch("seq") + Exchange.scratch("dp")
    return moving(
        kernel, number, operands, outs, [IN_VMEM] * len(outs), scratch, "return_grads", 110
    )


def sum_leading(ref):
    total = ref[0]
    for i in range(1, ref.shape[0]):
        total = total + ref[i]
    return total


def arrival(n_slow):
    lists = []
    for z in range(n_slow):
        near = sorted((t for t in range(n_slow) if t != z), key=lambda t: (abs(t - z), t))
        own = [(abs(t - z), 0, t) for t in near]
        side = [(abs(t - z) + 1.5, 1, t) for t in [z] + near]
        lists.append([(0, z)] + [(c, t) for _, c, t in sorted(own + side)])
    return lists


def look_up(tables, row, column):
    value = jnp.int32(0)
    for r, table in enumerate(tables):
        for c, entry in enumerate(table):
            if entry:
                value = value + jnp.where((row == r) & (column == c), entry, 0)
    return value


def expert_tiles(sw):
    tiles = []
    for e in range(EXP_DEV):
        for half in range(0, EF, 256):
            tiles.append((e, 2 * EF * e + half, 2 * EF * e + EF + half, EF * e + half, 256))
    tiles.append((None, 2 * EF * EXP_DEV, 2 * EF * EXP_DEV + sw, EF * EXP_DEV, sw))
    return tiles


def expert_pass(normed_two, cot_parts, up, down, router, number):
    n_dp = lax.axis_size("dp")
    experts = EXP_DEV * n_dp
    rows = normed_two.shape[0]
    wide, hidden = up.shape[1], down.shape[0]
    tiles = expert_tiles((wide - 2 * EF * EXP_DEV) // 2)
    part = cot_parts[0].shape[1]
    operands = [normed_two] + list(cot_parts) + [up, down, router]

    def kernel(
        nt, cot_a, cot_b, up, down, router, x_out, dj_out, hs_out, dx_out, out_out,
        x_all, cot, s_dj, s_hs, s_dx, s_out, g_send, g_recv, g_local, x_sem, c_sem, o_sem,
    ):
        loads = [
            pltpu.make_async_copy(some, cot.at[:, pl.ds(at, some.shape[1]), :], c_sem.at[i])
            for i, (some, at) in enumerate(((cot_a, 0), (cot_b, part)))
        ]
        for copy in loads:
            copy.start()
        greet(["dp"])
        me, slow, fast = place_in("dp")
        g = Gather("dp", nt, lambda block: x_all.at[block], g_send, g_recv, g_local)
        g.start()
        for copy in loads:
            copy.wait()
        g.settle()
        orders = arrival(g.n[0])
        sides = [[c for c, _ in order] for order in orders]
        places = [[t for _, t in order] for order in orders]

        def outgoing(slot, shard):
            return [
                pltpu.make_async_copy(held.at[slot], out.at[shard], o_sem.at[slot, i])
                for i, (held, out) in enumerate(
                    ((s_dj, dj_out), (s_hs, hs_out), (s_dx, dx_out), (s_out, out_out))
                )
            ]

        def body(i, carry):
            for t in range(1, g.n[0]):

                @pl.when(i == 2 * t - 1)
                def _():
                    g.relay(t)

            side = look_up(sides, slow, i)
            shard = look_up(places, slow, i) * 2 + fast + side * (1 - 2 * fast)

            @pl.when(side == 1)
            def _():
                g.copy(shard, 0).wait_recv()

            slot = i % 2

            @pl.when(i >= 2)
            def _():
                for copy in outgoing(slot, shard):
                    copy.wait()

            pltpu.make_async_copy(x_all.at[shard], x_out.at[shard], x_sem.at[i]).start()
            x = x_all[shard]
            c = cot[shard, :, :D]
            lane = lax.broadcasted_iota(jnp.int32, (1, LANES), 1)
            named = cot[shard, :, D:].astype(F32) > 0.0
            logits = dot(x, router[...])
            highest = jnp.max(jnp.where(named, logits, -1e30), 1, keepdims=True)
            raised = jnp.where(named, jnp.exp(logits - highest), 0.0)
            gates = raised / jnp.sum(raised, 1, keepdims=True)
            own = [
                jnp.sum(jnp.where(lane == EXP_DEV * me + e, gates, 0.0), 1, keepdims=True)
                for e in range(EXP_DEV)
            ]
            d_own = [jnp.zeros((rows, 1), F32) for _ in range(EXP_DEV)]
            for e, at_gate, at_up, at_down, w in tiles:
                gate = dot(x, up[:, at_gate : at_gate + w])
                lift = dot(x, up[:, at_up : at_up + w])
                d_hidden = dot_nt(c, down[at_down : at_down + w, :])
                sig = sigmoid(gate)
                silu = gate * sig
                h = (silu * lift).astype(BF).astype(F32)
                if e is None:
                    s_hs[slot, :, at_down : at_down + w] = h.astype(BF)
                else:
                    d_own[e] = d_own[e] + jnp.sum(h * d_hidden, 1, keepdims=True)
                    s_hs[slot, :, at_down : at_down + w] = (h * own[e]).astype(BF)
                    d_hidden = d_hidden * own[e]
                d_gate = d_hidden * lift * (sig * (1.0 + gate * (1.0 - sig)))
                s_dj[slot, :, at_gate : at_gate + w] = d_gate.astype(BF)
                s_dj[slot, :, at_up : at_up + w] = (d_hidden * silu).astype(BF)
            for n in range(0, D, 256):
                s_dx[slot, :, n : n + 256] = dot_nt(s_dj[slot], up[n : n + 256, :]).astype(BF)
                s_out[slot, :, n : n + 256] = dot(s_hs[slot], down[:, n : n + 256]).astype(BF)
            packed = jnp.zeros((rows, LANES), F32)
            for e in range(EXP_DEV):
                upper = d_own[e].astype(BF).astype(F32)
                at = EXP_DEV * me + e
                packed = packed + jnp.where(lane == at, upper, 0.0)
                packed = packed + jnp.where(lane == at + experts, d_own[e] - upper, 0.0)
            s_dx[slot, :, D:] = packed.astype(BF)
            for copy in outgoing(slot, shard):
                copy.start()
            return carry

        lax.fori_loop(0, n_dp, body, 0)
        for slot in range(2):
            for copy in outgoing(slot, 0):
                copy.wait()
        for i in range(n_dp):
            pltpu.make_async_copy(x_all.at[i], x_out.at[i], x_sem.at[i]).wait()
        g.drain(False)

    def blocks(width):
        return jax.ShapeDtypeStruct((n_dp, rows, width), BF)

    def held(width):
        return pltpu.VMEM((2, rows, width), BF)

    outs = [blocks(D), blocks(wide), blocks(hidden), blocks(D + LANES), blocks(D)]
    return pl.pallas_call(
        kernel,
        out_shape=outs,
        in_specs=[ANY] * 3 + [IN_VMEM] * 3,
        out_specs=[ANY] * len(outs),
        scratch_shapes=[
            pltpu.VMEM((n_dp, rows, D), BF),
            pltpu.VMEM((n_dp, rows, D + LANES), BF),
            held(wide), held(hidden), held(D + LANES), held(D),
        ]
        + Gather.scratch("dp")
        + [
            pltpu.SemaphoreType.DMA((n_dp,)),
            pltpu.SemaphoreType.DMA((2,)),
            pltpu.SemaphoreType.DMA((2, 4)),
        ],
        cost_estimate=pl.CostEstimate(
            flops=0, bytes_accessed=360 * 10**6, transcendentals=0
        ),
        compiler_params=pltpu.CompilerParams(
            collective_id=number, has_side_effects=True, vmem_limit_bytes=60 * 2**20
        ),
        name="expert_pass",
    )(*operands)


def sum_with_grads(d_x, x, d_joined, hidden, cot_parts, number):
    n_dp, rows, block_cols = d_x.shape
    total = n_dp * rows
    wide, deep = d_joined.shape[2], hidden.shape[2]
    main = 2 * EF * EXP_DEV
    part = cot_parts[0].shape[1]
    operands = [d_x, x, d_joined, hidden] + list(cot_parts)
    ups, downs = D // 256, deep // LANES

    def kernel(
        d_x, x_in, dj_in, hs_in, cot_a, cot_b, out, up_out, shared_out, down_out,
        x, dj, hs, cot, turned, low, s_up, s_down, l_sem, u_sem, d_sem, *scratch,
    ):
        loads = [
            pltpu.make_async_copy(x_in, x, l_sem.at[0]),
            pltpu.make_async_copy(dj_in, dj, l_sem.at[1]),
            pltpu.make_async_copy(hs_in, hs, l_sem.at[2]),
            pltpu.make_async_copy(cot_a, cot.at[:, pl.ds(0, part), :], l_sem.at[3]),
            pltpu.make_async_copy(cot_b, cot.at[:, pl.ds(part, rows - part), :], l_sem.at[4]),
        ]
        for copy in loads:
            copy.start()
        greet(["dp"])
        work = Scatter("dp", lambda target: d_x.at[target], out, *scratch)
        work.start()
        for copy in loads:
            copy.wait()

        def up_copies(slot, r):
            at = pl.ds(pl.multiple_of(r * 256, 256), 256)
            return [
                pltpu.make_async_copy(s_up.at[slot, :, pl.ds(0, main)], up_out.at[at], u_sem.at[slot, 0]),
                pltpu.make_async_copy(
                    s_up.at[slot, :, pl.ds(main, wide - main)], shared_out.at[at], u_sem.at[slot, 1]
                ),
            ]

        def down_copy(slot, r):
            at = pl.ds(pl.multiple_of(r * LANES, LANES), LANES)
            return pltpu.make_async_copy(s_down.at[slot], down_out.at[at], d_sem.at[slot])

        def up_body(r, carry):
            slot = r % 2

            @pl.when(r >= 2)
            def _():
                for copy in up_copies(slot, r):
                    copy.wait()

            at = pl.ds(pl.multiple_of(r * 256, 256), 256)
            for b in range(n_dp):
                turned[:, b * rows : (b + 1) * rows] = x[b, :, at].T

            def tile(c, inner):
                here = pl.ds(pl.multiple_of(c * 256, 256), 256)
                s_up[slot, :, here] = dot(
                    turned[...], dj[:, :, here].reshape(total, 256)
                ).astype(BF)
                return inner

            lax.fori_loop(0, wide // 256, tile, 0)
            for copy in up_copies(slot, r):
                copy.start()
            return carry

        def down_body(r, carry):
            slot = r % 2

            @pl.when(r >= 2)
            def _():
                down_copy(slot, r).wait()

            at = pl.ds(pl.multiple_of(r * LANES, LANES), LANES)
            for b in range(n_dp):
                low[:, b * rows : (b + 1) * rows] = hs[b, :, at].T

            def tile(c, inner):
                here = pl.ds(pl.multiple_of(c * 256, 256), 256)
                s_down[slot, :, here] = dot(
                    low[...], cot[:, :, here].reshape(total, 256)
                ).astype(BF)
                return inner

            lax.fori_loop(0, D // 256, tile, 0)
            down_copy(slot, r).start()
            return carry

        lax.fori_loop(0, 3, up_body, 0)
        work.step(0)
        lax.fori_loop(3, ups, up_body, 0)
        work.step(1)
        lax.fori_loop(0, downs // 2, down_body, 0)
        work.step(2)
        lax.fori_loop(downs // 2, downs, down_body, 0)
        for slot in range(2):
            for copy in up_copies(slot, 0):
                copy.wait()
            down_copy(slot, 0).wait()
        for k in range(3, work.steps()):
            work.step(k)
        work.drain()

    outs = [
        jax.ShapeDtypeStruct((rows, block_cols), F32),
        jax.ShapeDtypeStruct((D, main), BF),
        jax.ShapeDtypeStruct((D, wide - main), BF),
        jax.ShapeDtypeStruct((deep, D), BF),
    ]
    return pl.pallas_call(
        kernel,
        out_shape=outs,
        in_specs=[ANY] * len(operands),
        out_specs=[IN_VMEM, ANY, ANY, ANY],
        scratch_shapes=[
            pltpu.VMEM(x.shape, BF),
            pltpu.VMEM(d_joined.shape, BF),
            pltpu.VMEM(hidden.shape, BF),
            pltpu.VMEM((n_dp, rows, D + LANES), BF),
            pltpu.VMEM((256, total), BF),
            pltpu.VMEM((LANES, total), BF),
            pltpu.VMEM((2, 256, wide), BF),
            pltpu.VMEM((2, LANES, D), BF),
            pltpu.SemaphoreType.DMA((5,)),
            pltpu.SemaphoreType.DMA((2, 2)),
            pltpu.SemaphoreType.DMA((2,)),
        ]
        + Scatter.scratch("dp", (rows, block_cols), BF),
        cost_estimate=pl.CostEstimate(flops=0, bytes_accessed=280 * 10**6, transcendentals=0),
        compiler_params=pltpu.CompilerParams(
            collective_id=number, has_side_effects=True, vmem_limit_bytes=60 * 2**20
        ),
        name="sum_with_grads",
    )(*operands)


def pad_rows(pieces, rows=8):
    stacked = jnp.stack(pieces, 0)
    return jnp.pad(stacked, ((0, rows - stacked.shape[0]), (0, 0)))


def pad_lanes(v, width=LANES):
    return jnp.pad(v, ((0, 0),) * (v.ndim - 1) + ((0, width - v.shape[-1]),))


def matrix_rates():
    return (
        MATRIX_RATE * D ** (-0.5),
        MATRIX_RATE * (4 * D) ** (-0.5),
        MATRIX_RATE * D ** (-0.5),
        MATRIX_RATE * DI ** (-0.5),
        MATRIX_RATE * SF ** (-0.5),
        MATRIX_RATE * D ** (-0.5),
        MATRIX_RATE * (EF // TOPK) ** (-0.5),
    )


def adamw(weight, grad, first, second, rate, decay):
    first_new = BETA_ONE * first + (1.0 - BETA_ONE) * grad
    second_new = BETA_TWO * second + (1.0 - BETA_TWO) * grad * grad
    first_hat = first_new / (1.0 - BETA_ONE**STEP)
    second_hat = second_new / (1.0 - BETA_TWO**STEP)
    weight_new = weight - rate * (first_hat / (jnp.sqrt(second_hat) + ADAM_EPS) + decay * weight)
    return (weight_new, first_new, second_new)


def gather_rows(v, axis):
    return lax.all_gather(v, axis, axis=0, tiled=True)


def scatter_rows(v, axis):
    return lax.psum_scatter(v, axis, scatter_dimension=0, tiled=True)


def masked_gates(logits, mask):
    highest = jnp.max(jnp.where(mask > 0, logits, -jnp.inf), -1, keepdims=True)
    raised = jnp.where(mask > 0, jnp.exp(logits - highest), 0.0)
    return raised / jnp.sum(raised, -1, keepdims=True)


def experts_apart(normed_two_low, cot_all, up_full, down_full, router):
    n_dp = lax.axis_size("dp")
    at_dp = lax.axis_index("dp")
    experts = EXP_DEV * n_dp
    sw = down_full.shape[0] - EXP_DEV * EF
    cot_all = cot_all.reshape(-1, D + LANES)
    mask_all = cot_all[:, D : D + experts].astype(F32)
    cot_all = cot_all[:, :D]
    two_all = gather_blocks("dp", normed_two_low, 3, "gather_normed_two", 80).reshape(-1, D)
    gates_all = masked_gates(dot(two_all, router), mask_all)
    gates_own = lax.dynamic_slice_in_dim(gates_all, at_dp * EXP_DEV, EXP_DEV, 1)
    spread = jnp.concatenate(
        [
            jnp.broadcast_to(gates_own[:, 0:1], (gates_own.shape[0], EF)),
            jnp.broadcast_to(gates_own[:, 1:2], (gates_own.shape[0], EF)),
            jnp.ones((gates_own.shape[0], sw), F32),
        ],
        1,
    )
    joined = dot(two_all, up_full)
    gate_half = jnp.concatenate(
        [joined[:, :EF], joined[:, 2 * EF : 3 * EF], joined[:, 4 * EF : 4 * EF + sw]], 1
    )
    up_half = jnp.concatenate(
        [joined[:, EF : 2 * EF], joined[:, 3 * EF : 4 * EF], joined[:, 4 * EF + sw :]], 1
    )
    sig = jax.nn.sigmoid(gate_half)
    silu = gate_half * sig
    hidden = (silu * up_half).astype(BF).astype(F32)
    hidden_gated = (hidden * spread).astype(BF)
    moe_part = dot(hidden_gated, down_full).astype(BF)

    d_hidden = dot_nt(cot_all, down_full)
    touched = hidden * d_hidden
    d_gate_zero = jnp.sum(touched[:, :EF], 1)
    d_gate_one = jnp.sum(touched[:, EF : 2 * EF], 1)
    d_hidden = d_hidden * spread
    d_gate_half = (d_hidden * up_half * (sig * (1.0 + gate_half * (1.0 - sig)))).astype(BF)
    d_up_half = (d_hidden * silu).astype(BF)
    d_joined = jnp.concatenate(
        [
            d_gate_half[:, :EF],
            d_up_half[:, :EF],
            d_gate_half[:, EF : 2 * EF],
            d_up_half[:, EF : 2 * EF],
            d_gate_half[:, 2 * EF :],
            d_up_half[:, 2 * EF :],
        ],
        1,
    )
    grad_up = dot_tn(two_all, d_joined[:, : 4 * EF]).astype(BF)
    grad_shared = dot_tn(two_all, d_joined[:, 4 * EF :]).astype(BF)
    grad_down = dot_tn(hidden_gated, cot_all).astype(BF)
    expert_place = jnp.arange(experts)[None, :]
    d_gates = jnp.where(expert_place == at_dp * EXP_DEV, d_gate_zero[:, None], 0.0) + jnp.where(
        expert_place == at_dp * EXP_DEV + 1, d_gate_one[:, None], 0.0
    )
    returned = scatter_blocks(
        "dp",
        jnp.concatenate(
            [dot_nt(d_joined, up_full).astype(BF), pad_lanes(jnp.concatenate(split_two(d_gates), 1))],
            1,
        ).reshape(n_dp, -1, D + LANES),
        4,
        "sum_d_normed_two",
        80,
    )
    return returned, grad_up, grad_shared, grad_down, moe_part


def on_device(
    tokens,
    seg_flags,
    routes,
    out_grad,
    w_in,
    w_in_m,
    w_in_v,
    w_router,
    w_router_m,
    w_router_v,
    w_shared_in,
    w_shared_in_m,
    w_shared_in_v,
    w_out,
    w_out_m,
    w_out_v,
    w_shared_out,
    w_shared_out_m,
    w_shared_out_v,
    w_experts_in,
    w_experts_in_m,
    w_experts_in_v,
    w_experts_out,
    w_experts_out_m,
    w_experts_out_v,
    small_params,
    small_m,
    small_v,
):
    n_seq = lax.axis_size("seq")
    n_dp = lax.axis_size("dp")
    at_seq = lax.axis_index("seq")
    at_dp = lax.axis_index("dp")
    experts = EXP_DEV * n_dp
    length = seg_flags.shape[1]
    hl = HEADS // n_seq
    cl = hl * HEAD_DIM
    cc = cl + 2 * STATE
    rows_in = w_in.shape[0]
    rows_out = w_out.shape[0]
    shared_rows = w_shared_out.shape[0]
    x_local = tokens[0].astype(F32)
    cotangent = out_grad[0].astype(F32)
    gain_one, conv_weight, conv_bias, dt_bias, a_log, d_skip, gain_mix, gain_two = unpack(
        small_params
    )

    low_in = w_in.astype(BF)
    gate_part = low_in[:, :DI].reshape(rows_in, n_seq, cl)
    conv_part = low_in[:, DI : 2 * DI].reshape(rows_in, n_seq, cl)
    both_part = low_in[:, 2 * DI : 2 * DI + 2 * STATE]
    step_part = low_in[:, DI + XBC :].reshape(rows_in, n_seq, hl)
    tail_part = pad_lanes(
        jnp.concatenate(
            [step_part, jnp.broadcast_to(w_router.astype(BF)[:, None, :], (rows_in, n_seq, experts))],
            2,
        )
    )
    width = 2 * cl + 2 * STATE + LANES
    in_blocks = jnp.concatenate(
        [
            gate_part,
            conv_part,
            jnp.broadcast_to(both_part[:, None, :], (rows_in, n_seq, 2 * STATE)),
            tail_part,
        ],
        2,
    ).transpose(1, 0, 2)
    mask = jnp.sum(
        (routes[0][:, :, None] == jnp.arange(experts)[None, None, :]).astype(F32), 1
    )
    cot_rows = jnp.concatenate([out_grad[0], pad_lanes(mask.astype(BF))], 1)
    fused = plane("dp")[1] == 2
    early = cot_rows.shape[0] // 4 if fused else cot_rows.shape[0]
    cot_parts = [lax.all_gather(cot_rows[:early], "dp")]

    sw = n_seq * shared_rows
    shared_blocks = (
        w_shared_in.astype(BF)
        .reshape(rows_in, 2, n_seq, n_dp, shared_rows)
        .transpose(3, 0, 1, 2, 4)
        .reshape(n_dp, rows_in, 2 * sw)
    )
    e_low = w_experts_in.astype(BF)
    up_rows = jnp.concatenate([e_low[0], e_low[1]], 1)
    root_one = lax.rsqrt(jnp.mean(x_local * x_local, -1, keepdims=True) + EPS)
    normed_low = (x_local * root_one * gain_one).astype(BF)
    in_full, shared_full, out_full, normed_all, up_full, down_full, shared_down = bring_weights(
        in_blocks,
        shared_blocks,
        w_out.astype(BF),
        normed_low,
        up_rows,
        w_experts_out.astype(BF),
        w_shared_out.astype(BF),
        1,
    )
    if fused:
        late_rows, in_full = lax.optimization_barrier((cot_rows[early:], in_full))
        cot_parts.append(lax.all_gather(late_rows, "dp"))
    in_full = in_full.reshape(D, width)
    router = in_full[:, 2 * cl + 2 * STATE + hl : 2 * cl + 2 * STATE + hl + experts]
    out_full = out_full.reshape(cl, D)
    normed_all = normed_all.reshape(length, D)
    up_full = jnp.concatenate([up_full.reshape(D, 4 * EF), shared_full.reshape(D, 2 * sw)], 1)
    down_full = jnp.concatenate([down_full.reshape(2 * EF, D), shared_down.reshape(sw, D)], 0)
    ef_rows = w_experts_out.shape[1]

    projected = dot(normed_all, in_full)
    ids = jnp.cumsum(seg_flags[0])
    ids_behind = [
        jnp.concatenate([-jnp.ones((j,), ids.dtype), ids[: length - j]], 0) for j in range(KCONV)
    ]
    valid = [(behind == ids).astype(F32) for behind in ids_behind]
    cols = pad_lanes(jnp.stack(valid + [ids.astype(F32)], 1))
    rows = jnp.broadcast_to(
        ids.astype(F32).reshape(length // CHUNK, 1, CHUNK), (length // CHUNK, 8, CHUNK)
    )

    def local_channels(v):
        mine = lax.dynamic_slice_in_dim(v, at_seq * cl, cl, v.ndim - 1)
        return jnp.concatenate([mine, v[..., DI:]], -1)

    def local_heads(v):
        return lax.dynamic_slice_in_dim(v, at_seq * hl, hl)

    convp = jnp.pad(
        jnp.concatenate([local_channels(conv_weight), local_channels(conv_bias)[None]], 0),
        ((0, 8 - KCONV - 1), (0, 0)),
    )
    a_own = -jnp.exp(local_heads(a_log))
    headp = pad_rows([pad_lanes(local_heads(dt_bias)), pad_lanes(a_own)])
    chanp = pad_rows(
        [
            jnp.repeat(local_heads(d_skip), HEAD_DIM),
            lax.dynamic_slice_in_dim(gain_mix, at_seq * cl, cl),
        ]
    )
    gated_low, squares, mixer_out, states = mixer_forward(projected, cols, rows, convp, headp, chanp)
    mixed = scatter_blocks(
        "seq",
        jnp.concatenate(
            [dot(gated_low, out_full).astype(BF), pad_lanes(jnp.stack(split_two(squares[:, 0]), 1))],
            1,
        ).reshape(n_seq, length // n_seq, D + LANES),
        2,
        "sum_mixed",
        25,
    )
    square_sum = mixed[:, D : D + 1] + mixed[:, D + 1 : D + 2]
    mixed = mixed[:, :D]
    root_mix = lax.rsqrt(square_sum / DI + EPS)
    residual = x_local + root_mix * mixed
    root_two = lax.rsqrt(jnp.mean(residual * residual, -1, keepdims=True) + EPS)
    normed_two_low = (residual * root_two * gain_two).astype(BF)

    router_wide = pad_lanes(router)
    if fused:
        two_all, d_joined, hidden_gated, d_two, moe_part = expert_pass(
            normed_two_low, cot_parts, up_full, down_full, router_wide, 3
        )
        returned, grad_up, grad_shared, grad_down = sum_with_grads(
            d_two, two_all, d_joined, hidden_gated, cot_parts, 4
        )
    else:
        returned, grad_up, grad_shared, grad_down, moe_part = experts_apart(
            normed_two_low, cot_parts[0], up_full, down_full, router
        )
    if fused:
        moe_part, returned = lax.optimization_barrier((moe_part, returned))
    moe = scatter_rows(moe_part.reshape(-1, D), "dp")
    d_gates = returned[:, D : D + experts] + returned[:, D + experts : D + 2 * experts]
    gates = masked_gates(dot(normed_two_low, router), mask)
    d_logits = gates * (d_gates - jnp.sum(gates * d_gates, 1, keepdims=True))
    d_logits = d_logits.astype(BF)
    grad_router = dot_tn(normed_two_low, d_logits)
    d_normed_two = returned[:, :D] + dot_nt(d_logits, router)
    grad_gain_two = jnp.sum(d_normed_two * residual * root_two, 0)
    scaled = d_normed_two * gain_two
    d_residual = (
        cotangent
        + scaled * root_two
        - residual * (root_two**3 / D * jnp.sum(scaled * residual, -1, keepdims=True))
    )
    residual_low = d_residual.astype(BF)
    along = jnp.sum(residual_low.astype(F32) * mixed, 1)
    packed = jnp.stack(split_two(root_mix[:, 0]) + split_two(along), 1)
    residual_all = gather_blocks(
        "seq", jnp.concatenate([residual_low, pad_lanes(packed)], 1), 5, "gather_residual", 25
    ).reshape(length, D + LANES)
    packed = residual_all[:, D : D + 4].astype(F32)
    residual_all = residual_all[:, :D]
    cols_back = jnp.concatenate(
        [cols[:, :5], packed[:, 0:1] + packed[:, 1:2], packed[:, 2:3] + packed[:, 3:4], cols[:, 7:]], 1
    )
    d_mixer = dot_nt(residual_all, out_full)
    d_proj, mixer_low, d_conv, d_head, d_chan = mixer_backward(
        projected, cols_back, rows, convp, headp, chanp, mixer_out, states, d_mixer
    )
    grad_out = dot_tn(mixer_low, residual_all)
    d_normed = dot_nt(d_proj, in_full).astype(BF)
    if fused:
        d_normed, moe = lax.optimization_barrier((d_normed, moe))
    grad_in = dot_tn(normed_all, d_proj)
    grad_gain_one = jnp.sum(in_full.astype(F32) * grad_in, 1) / gain_one
    first_router = 2 * cl + 2 * STATE + hl
    grad_in = grad_in + jnp.pad(grad_router, ((0, 0), (first_router, width - first_router - experts)))

    def place_channels(v):
        base = jnp.zeros(v.shape[:-1] + (XBC,), F32)
        base = lax.dynamic_update_slice_in_dim(base, v[..., :cl], at_seq * cl, v.ndim - 1)
        return lax.dynamic_update_slice_in_dim(base, v[..., cl:], DI, v.ndim - 1)

    def place(v, whole):
        return lax.dynamic_update_slice_in_dim(
            jnp.zeros((whole,), F32), v, at_seq * v.shape[0], 0
        )

    small_local = jnp.concatenate(
        [
            grad_gain_one,
            place_channels(d_conv[:KCONV]).reshape(-1),
            place_channels(d_conv[KCONV]),
            place(d_head[0, :hl], HEADS),
            place(d_head[1, :hl], HEADS),
            place(jnp.sum(d_chan[0].reshape(hl, HEAD_DIM), 1), HEADS),
            place(d_chan[1], DI),
            grad_gain_two,
        ],
        0,
    )
    piece = -(-small_local.shape[0] // (n_dp * LANES * 8)) * 8
    small_blocks = jnp.pad(small_local, (0, n_dp * piece * LANES - small_local.shape[0]))
    (
        grad_in_own,
        grad_w_out,
        d_normed,
        grad_up_own,
        grad_w_experts_out,
        grad_shared_own,
        grad_w_shared_out,
        small_grad,
    ) = return_grads(
        grad_in.astype(BF).reshape(n_seq, n_dp, rows_in, width),
        grad_out.astype(BF).reshape(n_dp, rows_out, D),
        d_normed.reshape(n_seq, length // n_seq, D),
        grad_up.reshape(n_seq, D // n_seq, 4 * EF),
        grad_down[: 2 * EF].reshape(2, n_seq, ef_rows, D),
        grad_shared.reshape(n_seq, n_dp, rows_in, 2 * sw),
        grad_down[2 * EF :].reshape(n_seq, shared_rows, D),
        small_blocks.reshape(n_dp, piece, LANES),
        6,
    )
    grad_in_own = grad_in_own.astype(F32)
    grad_w_in = jnp.concatenate(
        [
            grad_in_own[:, :, :cl].transpose(1, 0, 2).reshape(rows_in, DI),
            grad_in_own[:, :, cl : 2 * cl].transpose(1, 0, 2).reshape(rows_in, DI),
            jnp.sum(grad_in_own[:, :, 2 * cl : 2 * cl + 2 * STATE], 0),
            grad_in_own[:, :, 2 * cl + 2 * STATE : first_router].transpose(1, 0, 2).reshape(rows_in, HEADS),
        ],
        1,
    )
    grad_w_router = jnp.sum(grad_in_own[:, :, first_router : first_router + experts], 0)
    grad_w_shared_in = (
        grad_shared_own.astype(F32)
        .reshape(n_dp, rows_in, 2, n_seq, shared_rows)
        .transpose(1, 2, 3, 0, 4)
        .reshape(rows_in, 2 * SF)
    )
    grad_w_experts_in = jnp.stack([grad_up_own[:, : 2 * EF], grad_up_own[:, 2 * EF :]], 0)
    small_grad = small_grad.reshape(-1)[: small_params.shape[0]]

    scaled = d_normed * gain_one
    input_grad = (
        d_residual
        + scaled * root_one
        - x_local * (root_one**3 / D * jnp.sum(scaled * x_local, -1, keepdims=True))
    )

    masters = (w_in, w_router, w_shared_in, w_out, w_shared_out, w_experts_in, w_experts_out)
    firsts = (
        w_in_m,
        w_router_m,
        w_shared_in_m,
        w_out_m,
        w_shared_out_m,
        w_experts_in_m,
        w_experts_out_m,
    )
    seconds = (
        w_in_v,
        w_router_v,
        w_shared_in_v,
        w_out_v,
        w_shared_out_v,
        w_experts_in_v,
        w_experts_out_v,
    )
    gradients = (
        grad_w_in,
        grad_w_router,
        grad_w_shared_in,
        grad_w_out,
        grad_w_shared_out,
        grad_w_experts_in,
        grad_w_experts_out,
    )
    rates = matrix_rates()
    block_out = (residual + moe.astype(F32)).astype(BF)
    results = [block_out[None], input_grad[None]]
    for member in range(7):
        results = results + list(
            adamw(
                masters[member],
                gradients[member],
                firsts[member],
                seconds[member],
                rates[member],
                DECAY_RATE,
            )
        )
    results = results + list(
        adamw(small_params, small_grad, small_m, small_v, SMALL_RATE, 0.0)
    )
    return tuple(results)


def solution(mesh):
    by_token = P("dp", "seq", None)
    dense = P(("seq", "dp"), None)
    expert = P("dp", "seq", None)
    weights = (dense,) * 15 + (expert,) * 6 + (P(),) * 3
    return jax.shard_map(
        on_device,
        mesh=mesh,
        in_specs=(by_token, P("dp", None), by_token, by_token) + weights,
        out_specs=(by_token, by_token) + weights,
        check_vma=False,
    )
```
